32 devices in a mesh: term: 8 (over y, x, core), sector: 4 (over z).
Axes of the slice: x: 2, y: 2, z: 4, core: 2. Of those that a mesh axis runs over, the one named last changes fastest.
Arguments:
- psi: float32 [8, 384, 4, 384], P('sector'), may hold values from -6 to 6
- precond: bfloat16 [8, 384, 4, 384], P('sector'), may hold values from 1 to 10
- left_environment_block: float32 [16, 8, 384, 384], P('term', 'sector'), may hold values from -0.3125 to 0.3125
- right_env: float32 [16, 8, 384, 384], P('term', 'sector'), may hold values from -0.3125 to 0.3125
- term_operators: float32 [16, 4, 4], P('term'), may hold values from -3 to 3
- term_charge: int32 [16], P('term'), may hold values from -1 to 1, as said below
- sector_sizes: int32 [8], P('sector'), may hold values from 128 to 384, as said below
- sector_energy: float32 [8], P('sector'), may hold values from 2 to 20
Outputs:
- psi_next: float32 [8, 384, 4, 384], P('sector', 'term')
- energies: float32 [1], replicated
The draws below stay inside these ranges and needn't reach their ends.
Inputs may be any that keep to these rules, and one draw needn't show every extreme that they name: `term_charge`: every value -1, 0 and 1 occurs. `sector_sizes`: some sector has exactly 384 states and some exactly 128.
All inputs are finite; a program needn't handle non-finite values.
Results may differ from the reference program's by a relative error of at most 0.0003.
Values sent between devices are 32-bit elements; how exact they have to be, the bound alone decides.
No kernel may reach another device: no remote copies, remote signals or barrier semaphores. Data moves between devices by JAX's collectives and lax.ppermute only.
A program may use at most 128 MiB of HBM per device.

```python
import math
import jax
import jax.numpy as jnp
from jax import lax

MS = 384
P_SIZE = 4
UPDATES = 1
TERMS = 16
SECTORS = 8


def draw_term_charge(key, part):
    charge = jax.random.randint(key, (TERMS,), -1, 2).astype(jnp.int32)
    picks = jax.random.permutation(jax.random.fold_in(key, 7), TERMS)
    charge = charge.at[picks[0]].set(-1)
    charge = charge.at[picks[1]].set(1)
    charge = charge.at[picks[2]].set(0)
    return charge.astype(jnp.int32)


def draw_sector_sizes(key, part):
    sizes = jax.random.randint(key, (SECTORS,), MS // 3, MS + 1).astype(jnp.int32)
    picks = jax.random.permutation(jax.random.fold_in(key, 11), SECTORS)
    sizes = sizes.at[picks[0]].set(MS)
    sizes = sizes.at[picks[1]].set(MS // 3)
    return sizes.astype(jnp.int32)


def shard_levels(own_key, shape, cuts, least, largest):
    def one(dim, parts):
        draws = jax.random.uniform(jax.random.fold_in(jax.random.fold_in(own_key, 6), dim), (parts,), jnp.float32, least / len(cuts), largest / len(cuts))
        return jnp.repeat(jnp.exp(draws), shape[dim] // parts).reshape((-1,) + (1,) * (len(shape) - dim - 1))

    gain = one(*cuts[0])
    for cut in cuts[1:]:
        gain = gain * one(*cut)
    return gain


def normal_values(stream_key, dims, scale, bound, shards=(), kind=jnp.bfloat16):
    entries = scale * jax.random.normal(stream_key, dims, jnp.float32)
    if shards:
        entries = entries * shard_levels(stream_key, dims, shards, -0.22, 0.18)
    return jnp.clip(entries, -bound, bound).astype(kind)


def setup_inputs(seed: int = 0) -> dict:
    key_list = jax.random.split(jax.random.key(seed), 9)
    return {
        "psi": normal_values(key_list[0], (SECTORS, MS, P_SIZE, MS), 1.0, 6.0, ((0, 4),), jnp.float32),
        "precond": jnp.clip(jnp.exp(math.log(10.0) - 2.3025851 * jax.random.uniform(key_list[1], (SECTORS, MS, P_SIZE, MS), jnp.float32) ** shard_levels(key_list[1], (SECTORS, MS, P_SIZE, MS), ((0, 4),), -0.2, 0.2)), 1.0, 10.0).astype(jnp.bfloat16),
        "left_environment_block": normal_values(key_list[2], (TERMS, SECTORS, MS, MS), MS ** -0.5, 0.3125, ((0, 8), (1, 4)), jnp.float32),
        "right_env": normal_values(key_list[3], (TERMS, SECTORS, MS, MS), MS ** -0.5, 0.3125, ((0, 8), (1, 4)), jnp.float32),
        "term_operators": normal_values(key_list[4], (TERMS, P_SIZE, P_SIZE), P_SIZE ** -0.5, 3.0, ((0, 8),), jnp.float32),
        "term_charge": draw_term_charge(jax.random.fold_in(key_list[8], 71), 0),
        "sector_sizes": draw_sector_sizes(jax.random.fold_in(key_list[8], 71), 0),
        "sector_energy": jnp.clip(jnp.exp(math.log(20.0) - 2.3025851 * jax.random.uniform(key_list[7], (SECTORS,), jnp.float32) ** shard_levels(key_list[7], (SECTORS,), ((0, 4),), -0.2, 0.2)), 2.0, 20.0),
    }


EPSILON = 1e-06
TOP_LEVEL = lax.Precision.HIGHEST

def hamiltonian(state, left_environment_block, right_env, term_operators, term_charge, sector_energy, valid_mask):
    zero_block = jnp.zeros_like(state[:1])
    from_below = jnp.concatenate([zero_block, state[:-1]], axis=0)
    from_above = jnp.concatenate([state[1:], zero_block], axis=0)

    def single_term(total, inputs):
        left_side, right, operator, charge = inputs
        source_sector = jnp.where(charge == 1, from_below, jnp.where(charge == -1, from_above, state))
        leading_item = jnp.einsum('qom,qmsg->qosg', left_side, source_sector, precision=TOP_LEVEL)
        second = jnp.einsum('pr,tarb->tapb', operator, leading_item, precision=TOP_LEVEL)
        third = jnp.einsum('tape,teb->tapb', second, right, precision=TOP_LEVEL)
        return (total + third, None)
    total, _ = lax.scan(single_term, jnp.zeros_like(state), (left_environment_block, right_env, term_operators, term_charge))
    return (total + sector_energy[:, None, None, None] * state) * valid_mask

def reference(psi, precond, left_environment_block, right_env, term_operators, term_charge, sector_sizes, sector_energy):
    positions = jnp.arange(MS, dtype=jnp.int32)
    inside = positions[None, :] < sector_sizes[:, None]
    valid_mask = (inside[:, :, None, None] & inside[:, None, None, :]).astype(jnp.float32)
    precond_wide = precond.astype(jnp.float32)
    state = psi * valid_mask
    energies = []
    for update_step in range(UPDATES):
        image = hamiltonian(state, left_environment_block, right_env, term_operators, term_charge, sector_energy, valid_mask)
        energy = jnp.sum(state * image) / jnp.sum(state * state)
        moved = state - (image - energy * state) / precond_wide
        state = moved * lax.rsqrt(jnp.mean(moved * moved) + EPSILON)
        energies.append(energy)
    return (state, jnp.stack(energies))
```

```python
import functools

import jax
import jax.numpy as jnp
from jax import lax
from jax.experimental import pallas as pl
from jax.experimental.pallas import tpu as pltpu
from jax.sharding import PartitionSpec as P

EPSILON = 1e-06
F32 = jnp.float32
BF16 = jnp.bfloat16
VMEM_BYTES = 56 * 1024 * 1024


def split(x):
    high = x.astype(BF16)
    return high, (x - high.astype(F32)).astype(BF16)


def dot(a, b):
    return jnp.dot(a, b, preferred_element_type=F32)


def row_tile(rows):
    return next(size for size in (64, 32, 16, 8) if rows % size == 0)


def split_into(src, high, low, first, rows, offset):
    tile = row_tile(rows)

    @pl.loop(0, rows // tile)
    def _(i):
        at = pl.ds(pl.multiple_of(first + i * tile, tile), tile)
        to = pl.ds(pl.multiple_of(offset + i * tile, tile), tile)
        a, b = split(src[at, :])
        high[to, :] = a
        low[to, :] = b


def pair_product(phys, operators, term, source, left, right, target, scratch):
    high, low = source
    stacked, product, mixed = scratch
    size = left.shape[0]
    part = right.shape[1]
    a, b = split(right[...])
    stacked[0:size, :] = a
    stacked[size : 2 * size, :] = b
    stacked[2 * size : 3 * size, :] = a

    @pl.loop(0, phys)
    def _(r):
        rows = pl.ds(pl.multiple_of(r * size, size), size)
        x, y = high[rows, :], low[rows, :]
        product[rows, :] = dot(jnp.concatenate([x, x, y], axis=1), stacked[...])

    tile = row_tile(size)

    @pl.loop(0, size // tile)
    def _(i):
        pieces = [
            product[pl.ds(pl.multiple_of(r * size + i * tile, tile), tile), :] for r in range(phys)
        ]
        for p in range(phys):
            total = operators[term, p * phys] * pieces[0]
            for r in range(1, phys):
                total = total + operators[term, p * phys + r] * pieces[r]
            x, y = split(total)
            cols = slice(p * part, (p + 1) * part)
            for place, value in enumerate((x, y, x)):
                at = pl.ds(pl.multiple_of(place * size + i * tile, tile), tile)
                mixed[at, cols] = value

    x, y = split(left[...])
    target[...] += dot(jnp.concatenate([x, x, y], axis=1), mixed[...])


def near_kernel(
    phys, charges, operators, own, left_a, left_b, right_a, right_b, out,
    raw, left, right, high, low, stacked, product, mixed, total, sems,
):
    sectors = own.shape[0]
    count = left_a.shape[0]
    loads = [
        pltpu.make_async_copy(own, raw, sems.at[0]),
        pltpu.make_async_copy(left_a, left.at[pl.ds(0, count)], sems.at[1]),
        pltpu.make_async_copy(right_a, right.at[pl.ds(0, count)], sems.at[2]),
        pltpu.make_async_copy(left_b, left.at[pl.ds(count, count)], sems.at[3]),
        pltpu.make_async_copy(right_b, right.at[pl.ds(count, count)], sems.at[4]),
    ]
    for load in loads:
        load.start()
    total[...] = jnp.zeros_like(total)
    loads[0].wait()
    for t in range(sectors):
        split_into(raw.at[t], high.at[t], low.at[t], 0, raw.shape[1], 0)
    for load in loads[1:]:
        load.wait()

    @pl.loop(0, 2 * count * sectors)
    def _(i):
        w = i // sectors
        t = i % sectors
        source = t - charges[w]

        @pl.when((source >= 0) & (source < sectors))
        def _():
            at = jnp.clip(source, 0, sectors - 1)
            pair_product(
                phys, operators, w, (high.at[at], low.at[at]), left.at[w, t], right.at[w, t],
                total.at[t], (stacked, product, mixed),
            )

    store = pltpu.make_async_copy(total, out, sems.at[0])
    store.start()
    store.wait()


def far_kernel(
    phys, chips, info, charges, operators, low_a, high_a, low_b, high_b, left_a, left_b, right_a,
    right_b, state, near, *refs,
):
    outs, products = refs[:chips], refs[chips]
    raw, left, right, high, low, stacked, product, mixed, total, here, sems, out_sems = refs[chips + 1 :]
    sectors = near.shape[0]
    count = left_a.shape[0]
    size = near.shape[1]
    half = size // 2
    rows = outs[0].shape[2]
    chip, core = info[0], info[1]
    loads = [
        pltpu.make_async_copy(low_a, raw.at[0, 0], sems.at[0]),
        pltpu.make_async_copy(high_a, raw.at[1, 0], sems.at[1]),
        pltpu.make_async_copy(low_b, raw.at[0, 1], sems.at[2]),
        pltpu.make_async_copy(high_b, raw.at[1, 1], sems.at[3]),
        pltpu.make_async_copy(left_a, left.at[pl.ds(0, count)], sems.at[4]),
        pltpu.make_async_copy(right_a, right.at[pl.ds(0, count)], sems.at[5]),
        pltpu.make_async_copy(left_b, left.at[pl.ds(count, count)], sems.at[6]),
        pltpu.make_async_copy(right_b, right.at[pl.ds(count, count)], sems.at[7]),
        pltpu.make_async_copy(near, total, sems.at[8]),
        pltpu.make_async_copy(state, here, sems.at[9]),
    ]
    for load in loads:
        load.start()
    for place in range(2):
        for side in range(2):
            loads[2 * place + side].wait()
            offset = (core if place == 0 else 1 - core) * half
            for r in range(phys):
                split_into(
                    raw.at[side, place], high.at[side], low.at[side], r * half, half, r * size + offset
                )
    for load in loads[4:]:
        load.wait()

    @pl.loop(0, 2 * count)
    def _(w):
        charge = charges[w]

        @pl.when(charge != 0)
        def _():
            side = jnp.where(charge > 0, 0, 1)
            t = jnp.where(charge > 0, 0, sectors - 1)
            pair_product(
                phys, operators, w, (high.at[side], low.at[side]), left.at[w, t], right.at[w, t],
                total.at[t], (stacked, product, mixed),
            )

    stores = []
    for j in range(chips):
        for c in range(2):
            first = pl.multiple_of((2 * (chip ^ j) + (core ^ c)) * rows, rows)
            stores.append(
                pltpu.make_async_copy(
                    total.at[:, pl.ds(first, rows), :], outs[j].at[:, c], out_sems.at[2 * j + c]
                )
            )
    for store in stores:
        store.start()
    tile = row_tile(size)
    products[...] = jnp.zeros_like(products)
    for t in range(sectors):

        @pl.loop(0, size // tile)
        def _(i):
            at = pl.ds(pl.multiple_of(i * tile, tile), tile)
            x = total[t, at, :] * here[t, at, :]
            products[...] += jnp.sum(x.reshape(tile // 8, 8, x.shape[1]), axis=0)

    for store in stores:
        store.wait()


def swap_cores(x, count):
    return lax.ppermute(x, "term", [(i, i ^ 1) for i in range(count)])


def sum_everywhere(x, axes):
    for axis in axes:
        count = lax.axis_size(axis)
        if count & (count - 1):
            x = lax.psum(x, axis)
            continue
        bit = 1
        while bit < count:
            x = x + lax.ppermute(x, axis, [(i, i ^ bit) for i in range(count)])
            bit *= 2
    return x


def body(
    psi, precond, left_environment_block, right_env, term_operators, term_charge, sector_sizes,
    sector_energy,
):
    sectors, size, phys, _ = psi.shape
    terms = term_charge.shape[0]
    count, planes = lax.axis_size("term"), lax.axis_size("sector")
    chips = count // 2
    rows = size // count
    half = size // 2
    lanes = phys * half
    numel = sectors * planes * size * phys * size
    me = lax.axis_index("term")
    chip, core = me // 2, me % 2

    positions = jnp.arange(size, dtype=jnp.int32)
    inside = positions[None, :] < sector_sizes[:, None]

    def masked(x, row_first, row_count, col_first, col_count):
        x = lax.dynamic_slice(x, (0, row_first, 0, col_first), (sectors, row_count, phys, col_count))
        a = lax.dynamic_slice(inside, (0, row_first), (sectors, row_count))
        b = lax.dynamic_slice(inside, (0, col_first), (sectors, col_count))
        return jnp.where(a[:, :, None, None] & b[:, None, None, :], x, 0)

    sent = masked(psi, core * half, half, 0, size)
    forward = [(i, i + 1) for i in range(planes - 1)]
    backward = [(b, a) for a, b in forward]

    def flat(x):
        return jnp.transpose(x, (1, 0, 2)).reshape(phys * half, size)

    low_a = lax.ppermute(flat(sent[sectors - 1]), "sector", forward)
    high_a = lax.ppermute(flat(sent[0]), "sector", backward)
    low_b = swap_cores(low_a, count)
    high_b = swap_cores(high_a, count)

    left_a = left_environment_block
    left_b = swap_cores(left_a, count)
    right_a = lax.dynamic_slice_in_dim(right_env, core * half, half, 3)
    right_b = swap_cores(lax.dynamic_slice_in_dim(right_env, (1 - core) * half, half, 3), count)
    small = jnp.concatenate(
        [term_operators.reshape(terms, phys * phys), term_charge.astype(F32)[:, None]], axis=1
    )
    small = jnp.concatenate([small, swap_cores(small, count)], axis=0)
    operators = small[:, : phys * phys]
    charges = small[:, phys * phys].astype(jnp.int32)

    own = jnp.transpose(masked(psi, 0, size, 0, size), (0, 2, 1, 3)).reshape(sectors, phys * size, size)
    state_half = masked(psi, 0, size, core * half, half).reshape(sectors, size, lanes)

    any_spec = pl.BlockSpec(memory_space=pl.ANY)
    smem = pl.BlockSpec(memory_space=pltpu.SMEM)
    pair_scratch = [
        pltpu.VMEM((3 * size, half), BF16),
        pltpu.VMEM((phys * size, half), F32),
        pltpu.VMEM((3 * size, lanes), BF16),
        pltpu.VMEM((sectors, size, lanes), F32),
    ]
    env_scratch = [
        pltpu.VMEM((2 * terms, sectors, size, size), F32),
        pltpu.VMEM((2 * terms, sectors, size, half), F32),
    ]
    params = pltpu.CompilerParams(vmem_limit_bytes=VMEM_BYTES)
    near = pl.pallas_call(
        functools.partial(near_kernel, phys),
        out_shape=jax.ShapeDtypeStruct((sectors, size, lanes), F32),
        in_specs=[smem] * 2 + [any_spec] * 5,
        out_specs=any_spec,
        scratch_shapes=[
            pltpu.VMEM((sectors, phys * size, size), F32),
            *env_scratch,
            pltpu.VMEM((sectors, phys * size, size), BF16),
            pltpu.VMEM((sectors, phys * size, size), BF16),
            *pair_scratch,
            pltpu.SemaphoreType.DMA((5,)),
        ],
        compiler_params=params,
        cost_estimate=pl.CostEstimate(
            flops=12 * terms * sectors * size * size * lanes, bytes_accessed=16 << 20, transcendentals=0
        ),
        name="near_terms",
    )(charges, operators, own, left_a, left_b, right_a, right_b)

    info = jnp.stack([chip, core]).astype(jnp.int32)
    block = jax.ShapeDtypeStruct((sectors, 2, rows, lanes), F32)
    results = pl.pallas_call(
        functools.partial(far_kernel, phys, chips),
        out_shape=[block] * chips + [jax.ShapeDtypeStruct((8, lanes), F32)],
        in_specs=[smem] * 3 + [any_spec] * 10,
        out_specs=[any_spec] * chips + [pl.BlockSpec(memory_space=pltpu.VMEM)],
        scratch_shapes=[
            pltpu.VMEM((2, 2, phys * half, size), F32),
            *env_scratch,
            pltpu.VMEM((2, phys * size, size), BF16),
            pltpu.VMEM((2, phys * size, size), BF16),
            *pair_scratch,
            pltpu.VMEM((sectors, size, lanes), F32),
            pltpu.SemaphoreType.DMA((10,)),
            pltpu.SemaphoreType.DMA((2 * chips,)),
        ],
        compiler_params=params,
        cost_estimate=pl.CostEstimate(
            flops=6 * terms * sectors * size * size * lanes, bytes_accessed=16 << 20, transcendentals=0
        ),
        name="far_terms",
    )(
        info, charges, operators, low_a, high_a, low_b, high_b, left_a, left_b, right_a, right_b,
        state_half, near,
    )
    parts, overlap = results[:chips], results[chips]

    def share(x):
        x = x.reshape(sectors, 2, rows, lanes)
        return jnp.where(core == 0, x, x[:, ::-1])

    first = chip * 2 * rows
    state = share(masked(psi, first, 2 * rows, core * half, half))
    scale = share(masked(1.0 / precond.astype(F32), first, 2 * rows, core * half, half))
    squares = jnp.sum(state * state, axis=(1, 2, 3))
    sums = jnp.stack(
        [
            jnp.sum(overlap) + jnp.sum(sector_energy * squares),
            jnp.sum(squares),
        ]
    )
    sums = sum_everywhere(sums, ("term", "sector"))
    energy = sums[0] / sums[1]

    total = parts[0]
    for j in range(1, chips):
        total = total + lax.ppermute(parts[j], "term", [(i, i ^ (2 * j)) for i in range(count)])
    shift = sector_energy - energy
    moved = state - (total + shift[:, None, None, None] * state) * scale
    square = sum_everywhere(jnp.sum(moved * moved), ("term", "sector"))

    mine = moved[:, 0].reshape(sectors, rows, phys, half)
    other = swap_cores(moved[:, 1], count).reshape(sectors, rows, phys, half)
    both = jnp.where(
        core == 0, jnp.concatenate([mine, other], axis=3), jnp.concatenate([other, mine], axis=3)
    )
    return both * lax.rsqrt(square / numel + EPSILON), jnp.stack([energy])


def solution(mesh):
    in_specs = (
        P("sector", None, None, None),
        P("sector", None, None, None),
        P("term", "sector", None, None),
        P("term", "sector", None, None),
        P("term", None, None),
        P("term"),
        P("sector"),
        P("sector"),
    )
    out_specs = (P("sector", "term", None, None), P())
    return jax.shard_map(body, mesh=mesh, in_specs=in_specs, out_specs=out_specs, check_vma=False)
```

```python
import functools

import jax
import jax.numpy as jnp
from jax import lax
from jax.experimental import pallas as pl
from jax.experimental.pallas import tpu as pltpu
from jax.sharding import PartitionSpec as P

EPSILON = 1e-06
F32 = jnp.float32
BF16 = jnp.bfloat16
VMEM_BYTES = 56 * 1024 * 1024


def split(x):
    high = x.astype(BF16)
    return high, (x - high.astype(F32)).astype(BF16)


def dot(a, b):
    return jnp.dot(a, b, preferred_element_type=F32)


def row_tile(rows):
    return next(size for size in (64, 32, 16, 8) if rows % size == 0)


def rows_at(first, count):
    return pl.ds(pl.multiple_of(first, count), count)


def start(copies):
    for copy in copies:
        copy.start()


def wait(copies):
    for copy in copies:
        copy.wait()


def load_blocks(src, dst, rows, sems):
    return [
        pltpu.make_async_copy(src.at[:, r, :], dst.at[pl.ds(r * rows, rows), :], sems.at[r])
        for r in range(src.shape[1])
    ]


def split_rows(src, high, low):
    tile = row_tile(src.shape[0])

    @pl.loop(0, src.shape[0] // tile)
    def _(i):
        at = rows_at(i * tile, tile)
        a, b = split(src[at, :])
        high[at, :] = a
        low[at, :] = b


def split_half(core, src, stacked):
    size, half = src.shape[0], stacked.shape[1]
    for side in range(2):

        @pl.when(core == side)
        def _():
            a, b = split(src[:, side * half : (side + 1) * half])
            stacked[0:size, :] = a
            stacked[size : 2 * size, :] = b
            stacked[2 * size : 3 * size, :] = a


def first_product(high, low, stacked, product):
    x, y = high[...], low[...]
    product[...] = dot(jnp.concatenate([x, x, y], axis=1), stacked[...])


def mix(operator, product, store):
    phys = operator.shape[0]
    rows = product.shape[0] // phys
    tile = row_tile(rows)

    @pl.loop(0, rows // tile)
    def _(i):
        pieces = [product[rows_at(r * rows + i * tile, tile), :] for r in range(phys)]
        for p in range(phys):
            total = operator[p, 0] * pieces[0]
            for r in range(1, phys):
                total = total + operator[p, r] * pieces[r]
            store(i * tile, tile, p, *split(total))


def second_product(left, mixed, target):
    x, y = split(left[...])
    target[...] += dot(jnp.concatenate([x, x, y], axis=1), mixed[...])


def near_kernel(
    first_call, phys, chips, info, sizes, charges, operators, *refs,
):
    if first_call:
        energies, psi, left_in, right_in, out, state_out, share_out, squares = refs[:8]
        raw, left, right, high, low, stacked, product, mixed, total, state, sems = refs[8:]
    else:
        psi, left_in, right_in, base, out = refs[:5]
        raw, left, right, high, low, stacked, product, mixed, total, sems = refs[5:]
    chip, core = info[0], info[1]
    sectors, size = psi.shape[0], psi.shape[1]
    count = left.shape[0]
    half = size // 2
    loads = []
    for t in range(sectors):
        loads += load_blocks(psi.at[t], raw.at[t], size, sems.at[t])
    loads += [
        pltpu.make_async_copy(right_in, right, sems.at[sectors, 0]),
        pltpu.make_async_copy(left_in, left, sems.at[sectors, 1]),
    ]
    if not first_call:
        loads.append(pltpu.make_async_copy(base, total, sems.at[sectors, 2]))
    start(loads)
    wait(loads[: sectors * phys])
    tile = row_tile(size)
    if first_call:
        squares[...] = jnp.zeros_like(squares)
    for t in range(sectors):
        limit = sizes[t]
        columns = lax.broadcasted_iota(jnp.int32, (tile, size), 1)
        lines = lax.broadcasted_iota(jnp.int32, (tile, size), 0)

        @pl.loop(0, size // tile)
        def _(i):
            keep = (columns < limit) & (lines + i * tile < limit)
            for r in range(phys):
                at = rows_at(r * size + i * tile, tile)
                x = jnp.where(keep, raw[t, at, :], 0)
                a, b = split(x)
                high[t, at, :] = a
                low[t, at, :] = b
                if first_call:
                    for side in range(2):

                        @pl.when(core == side)
                        def _():
                            state[t, rows_at(i * tile, tile), r * half : (r + 1) * half] = x[
                                :, side * half : (side + 1) * half
                            ]

            if first_call:
                x = state[t, rows_at(i * tile, tile), :]
                total[t, rows_at(i * tile, tile), :] = x * (energies[t] * (1.0 / chips))
                squares[...] += jnp.sum((x * x).reshape(tile // 8, 8, x.shape[1]), axis=0)

    stores = []
    if first_call:
        rows = share_out.shape[2]
        stores.append(pltpu.make_async_copy(state, state_out, sems.at[0, 0]))
        for c in range(2):
            at = rows_at((2 * chip + (core ^ c)) * rows, rows)
            stores.append(
                pltpu.make_async_copy(state.at[:, at, :], share_out.at[:, c], sems.at[0, c + 1])
            )
        start(stores)
    wait(loads[sectors * phys :])

    @pl.loop(0, count * sectors)
    def _(i):
        w = i // sectors
        t = i % sectors
        source = t - charges[w]

        @pl.when((source >= 0) & (source < sectors))
        def _():
            at = jnp.clip(source, 0, sectors - 1)
            split_half(core, right.at[w, t], stacked)
            first_product(high.at[at], low.at[at], stacked, product)

            def store(first, tile, p, a, b):
                cols = slice(p * half, (p + 1) * half)
                for place, value in enumerate((a, b, a)):
                    mixed[rows_at(place * size + first, tile), cols] = value

            mix(operators.at[w], product, store)
            second_product(left.at[w, t], mixed, total.at[t])

    last = pltpu.make_async_copy(total, out, sems.at[sectors, 0])
    last.start()
    wait(stores)
    last.wait()


def far_products(core, charges, operators, halo, right, raw, high, low, stacked, product, sems, loads, store):
    half = halo[0].shape[0]
    wait(loads)
    for side in range(2):
        split_rows(raw.at[side], high.at[side], low.at[side])
    for group in range(2):
        count = charges[group].shape[0]

        @pl.loop(0, count)
        def _(w):
            charge = charges[group][w]

            @pl.when(charge != 0)
            def _():
                side = jnp.where(charge > 0, 0, 1)
                split_half(core, right.at[group * count + w], stacked)
                first_product(high.at[side], low.at[side], stacked, product)
                mix(operators[group].at[w], product, functools.partial(store, group * count + w))


def end_target(charge, sectors):
    return jnp.where(charge > 0, 0, sectors - 1)


def load_ends(charges, source, target, sems):
    copies = []
    for group in range(2):
        count, sectors = source[group].shape[:2]
        for w in range(count):
            t = end_target(charges[group][w], sectors)
            copies.append(
                pltpu.make_async_copy(
                    source[group].at[w, t], target.at[group * count + w], sems.at[group * count + w]
                )
            )
    return copies


def far_first_kernel(
    phys, info, charges_a, charges_b, operators_a, operators_b, low_in, high_in, right_a, right_b, out,
    raw, right, high, low, stacked, product, mixed, sems,
):
    core = info[1]
    half = low_in.shape[0]
    charges, operators = (charges_a, charges_b), (operators_a, operators_b)
    loads = load_blocks(low_in, raw.at[0], half, sems.at[0])
    loads += load_blocks(high_in, raw.at[1], half, sems.at[1])
    loads += load_ends(charges, (right_a, right_b), right, sems.at[2])
    start(loads)

    def store(w, first, tile, p, a, b):
        cols = slice(p * half, (p + 1) * half)
        mixed[w, 0, rows_at(first, tile), cols] = a
        mixed[w, 1, rows_at(first, tile), cols] = b

    far_products(
        core, charges, operators, (low_in, high_in), right, raw, high, low, stacked, product, sems, loads, store
    )
    last = pltpu.make_async_copy(mixed, out, sems.at[0, 0])
    last.start()
    last.wait()


def far_last_kernel(
    phys, chips, info, charges_a, charges_b, operators_a, operators_b, low_in, high_in, right_a, right_b,
    left_a, left_b, state, near, early, *refs,
):
    outs, products = refs[:chips], refs[chips]
    raw, right, left, high, low, stacked, product, mixed, total, here, sems, out_sems = refs[chips + 1 :]
    chip, core = info[0], info[1]
    half = low_in.shape[0]
    size = 2 * half
    sectors = near.shape[0]
    rows = outs[0].shape[2]
    terms = right.shape[0]
    charges, operators = (charges_a, charges_b), (operators_a, operators_b)
    loads = load_blocks(low_in, raw.at[0], half, sems.at[0])
    loads += load_blocks(high_in, raw.at[1], half, sems.at[1])
    loads += load_ends(charges, (right_a, right_b), right, sems.at[2])
    more = []
    for w in range(terms):
        for place, part in enumerate((0, 1, 0)):
            more.append(
                pltpu.make_async_copy(
                    early.at[w, part],
                    mixed.at[w, rows_at(place * size + core * half, half), :],
                    sems.at[3 + place, w],
                )
            )
    more += load_ends(charges, (left_a, left_b), left, sems.at[6])
    more.append(pltpu.make_async_copy(near, total, sems.at[7, 0]))
    more.append(pltpu.make_async_copy(state, here, sems.at[7, 1]))
    start(loads + more)

    def store(w, first, tile, p, a, b):
        cols = slice(p * half, (p + 1) * half)
        for place, value in enumerate((a, b, a)):
            mixed[w, rows_at(place * size + (1 - core) * half + first, tile), cols] = value

    far_products(
        core, charges, operators, (low_in, high_in), right, raw, high, low, stacked, product, sems, loads, store
    )
    wait(more)
    for group in range(2):
        count = charges[group].shape[0]

        @pl.loop(0, count)
        def _(w):
            charge = charges[group][w]

            @pl.when(charge != 0)
            def _():
                t = end_target(charge, sectors)
                at = group * count + w
                second_product(left.at[at], mixed.at[at], total.at[t])

    stores = []
    for j in range(chips):
        for c in range(2):
            first = (2 * (chip ^ j) + (core ^ c)) * rows
            stores.append(
                pltpu.make_async_copy(
                    total.at[:, rows_at(first, rows), :], outs[j].at[:, c], out_sems.at[2 * j + c]
                )
            )
    start(stores)
    tile = row_tile(size)
    products[...] = jnp.zeros_like(products)
    for t in range(sectors):

        @pl.loop(0, size // tile)
        def _(i):
            at = rows_at(i * tile, tile)
            x = total[t, at, :] * here[t, at, :]
            products[...] += jnp.sum(x.reshape(tile // 8, 8, x.shape[1]), axis=0)

    wait(stores)


def swap_cores(x, count):
    return lax.ppermute(x, "term", [(i, i ^ 1) for i in range(count)])


def exchange_sum(x, axis, steps):
    count = lax.axis_size(axis)
    parts = [lax.ppermute(x, axis, [(i, i ^ step) for i in range(count)]) for step in steps]
    return sum(parts, x)


def doublings(count, first=1):
    steps = []
    while first < count:
        steps.append(first)
        first *= 2
    return steps


def body(
    psi, precond, left_environment_block, right_env, term_operators, term_charge, sector_sizes,
    sector_energy,
):
    sectors, size, phys, _ = psi.shape
    terms = term_charge.shape[0]
    count, planes = lax.axis_size("term"), lax.axis_size("sector")
    chips = count // 2
    rows = size // count
    half = size // 2
    lanes = phys * half
    numel = sectors * planes * size * phys * size
    me = lax.axis_index("term")
    chip, core = me // 2, me % 2
    info = jnp.stack([chip, core]).astype(jnp.int32)

    positions = jnp.arange(size, dtype=jnp.int32)

    def edge(t):
        limit = sector_sizes[t]
        x = lax.dynamic_slice_in_dim(psi[t], core * half, half, 0)
        a = core * half + jnp.arange(half, dtype=jnp.int32) < limit
        b = positions < limit
        return jnp.where(a[:, None, None] & b[None, None, :], x, 0)

    forward = [(i, i + 1) for i in range(planes - 1)]
    backward = [(b, a) for a, b in forward]
    low_a = lax.ppermute(edge(sectors - 1), "sector", forward)
    high_a = lax.ppermute(edge(0), "sector", backward)

    left_a, right_a, charges_a, operators_a = left_environment_block, right_env, term_charge, term_operators
    charges_b = swap_cores(charges_a, count)
    operators_b = swap_cores(operators_a, count)
    right_b = swap_cores(right_a, count)
    left_b = swap_cores(left_a, count)

    any_spec = pl.BlockSpec(memory_space=pl.ANY)
    smem = pl.BlockSpec(memory_space=pltpu.SMEM)
    vmem = pl.BlockSpec(memory_space=pltpu.VMEM)
    params = pltpu.CompilerParams(vmem_limit_bytes=VMEM_BYTES)
    wide = jax.ShapeDtypeStruct((sectors, size, lanes), F32)
    block = jax.ShapeDtypeStruct((sectors, 2, rows, lanes), F32)
    sums = jax.ShapeDtypeStruct((8, lanes), F32)
    near_scratch = [
        pltpu.VMEM((sectors, phys * size, size), F32),
        pltpu.VMEM((terms, sectors, size, size), F32),
        pltpu.VMEM((terms, sectors, size, size), F32),
        pltpu.VMEM((sectors, phys * size, size), BF16),
        pltpu.VMEM((sectors, phys * size, size), BF16),
        pltpu.VMEM((3 * size, half), BF16),
        pltpu.VMEM((phys * size, half), F32),
        pltpu.VMEM((3 * size, lanes), BF16),
        pltpu.VMEM((sectors, size, lanes), F32),
    ]
    near_sems = pltpu.SemaphoreType.DMA((sectors + 1, max(phys, 4)))

    def cost(pairs):
        return pl.CostEstimate(
            flops=pairs * 3 * 4 * size * size * lanes, bytes_accessed=12 << 20, transcendentals=0
        )

    near, state_half, state, squares = pl.pallas_call(
        functools.partial(near_kernel, True, phys, chips),
        out_shape=[wide, wide, block, sums],
        in_specs=[smem] * 5 + [any_spec] * 3,
        out_specs=[any_spec] * 3 + [vmem],
        scratch_shapes=[*near_scratch, pltpu.VMEM((sectors, size, lanes), F32), near_sems],
        compiler_params=params,
        cost_estimate=cost(terms * sectors),
        name="near_own",
    )(info, sector_sizes, charges_a, operators_a, sector_energy, psi, left_a, right_a)
    near = pl.pallas_call(
        functools.partial(near_kernel, False, phys, chips),
        out_shape=wide,
        in_specs=[smem] * 4 + [any_spec] * 4,
        out_specs=any_spec,
        scratch_shapes=[*near_scratch, near_sems],
        compiler_params=params,
        cost_estimate=cost(terms * sectors),
        name="near_partner",
    )(info, sector_sizes, charges_b, operators_b, psi, left_b, right_b, near)

    first = chip * 2 * rows
    scale = lax.dynamic_slice(
        precond, (0, first, 0, core * half), (sectors, 2 * rows, phys, half)
    ).astype(F32)
    inside = positions[None, :] < sector_sizes[:, None]
    a = lax.dynamic_slice(inside, (0, first), (sectors, 2 * rows))
    b = lax.dynamic_slice(inside, (0, core * half), (sectors, half))
    scale = jnp.where(a[:, :, None, None] & b[:, None, None, :], 1.0 / scale, 0)
    scale = scale.reshape(sectors, 2, rows, lanes)
    scale = jnp.where(core == 0, scale, scale[:, ::-1])

    low_a, high_a, near, scale = lax.optimization_barrier((low_a, high_a, near, scale))
    low_b = swap_cores(low_a, count)
    high_b = swap_cores(high_a, count)

    far_scratch = [
        pltpu.VMEM((2, phys * half, size), BF16),
        pltpu.VMEM((2, phys * half, size), BF16),
        pltpu.VMEM((3 * size, half), BF16),
        pltpu.VMEM((phys * half, half), F32),
    ]
    raw = pltpu.VMEM((2, phys * half, size), F32)
    ends = pltpu.VMEM((2 * terms, size, size), F32)
    far_sems = pltpu.SemaphoreType.DMA((8, max(phys, 2 * terms)))
    early = pl.pallas_call(
        functools.partial(far_first_kernel, phys),
        out_shape=jax.ShapeDtypeStruct((2 * terms, 2, half, lanes), BF16),
        in_specs=[smem] * 5 + [any_spec] * 4,
        out_specs=any_spec,
        scratch_shapes=[raw, ends, *far_scratch, pltpu.VMEM((2 * terms, 2, half, lanes), BF16), far_sems],
        compiler_params=params,
        cost_estimate=cost(terms // 2),
        name="far_first",
    )(info, charges_a, charges_b, operators_a, operators_b, low_a, high_a, right_a, right_b)

    results = pl.pallas_call(
        functools.partial(far_last_kernel, phys, chips),
        out_shape=[block] * chips + [sums],
        in_specs=[smem] * 5 + [any_spec] * 9,
        out_specs=[any_spec] * chips + [vmem],
        scratch_shapes=[
            raw,
            ends,
            ends,
            *far_scratch,
            pltpu.VMEM((2 * terms, 3 * size, lanes), BF16),
            pltpu.VMEM((sectors, size, lanes), F32),
            pltpu.VMEM((sectors, size, lanes), F32),
            far_sems,
            pltpu.SemaphoreType.DMA((2 * chips,)),
        ],
        compiler_params=params,
        cost_estimate=cost(terms),
        name="far_last",
    )(
        info, charges_a, charges_b, operators_a, operators_b, low_b, high_b, right_a, right_b, left_a, left_b,
        state_half, near, early,
    )
    parts, overlap = results[:chips], results[chips]

    arrived = [
        lax.ppermute(parts[j], "term", [(i, i ^ (2 * j)) for i in range(count)]) for j in range(1, chips)
    ]
    both = jnp.stack([jnp.sum(overlap), jnp.sum(squares) / chips])
    for step in doublings(planes):
        both = exchange_sum(both, "sector", [step])
    both = exchange_sum(both, "term", [1])
    both = exchange_sum(both, "term", [2 * j for j in range(1, chips)])
    energy = both[0] / both[1]

    total = sum(arrived, parts[0])
    moved = state - (total - energy * state) * scale
    other = swap_cores(moved[:, 1], count)
    devices = count * planes
    square = jnp.broadcast_to(jnp.sum(moved * moved), (devices, 128))
    square = lax.all_to_all(square, ("sector", "term"), 0, 0, tiled=True)
    square = jnp.sum(square[:, 0])

    mine = moved[:, 0].reshape(sectors, rows, phys, half)
    other = other.reshape(sectors, rows, phys, half)
    whole = jnp.where(
        core == 0, jnp.concatenate([mine, other], axis=3), jnp.concatenate([other, mine], axis=3)
    )
    return whole * lax.rsqrt(square / numel + EPSILON), jnp.stack([energy])


def solution(mesh):
    in_specs = (
        P("sector", None, None, None),
        P("sector", None, None, None),
        P("term", "sector", None, None),
        P("term", "sector", None, None),
        P("term", None, None),
        P("term"),
        P("sector"),
        P("sector"),
    )
    out_specs = (P("sector", "term", None, None), P())
    return jax.shard_map(body, mesh=mesh, in_specs=in_specs, out_specs=out_specs, check_vma=False)
```

```python
import functools

import jax
import jax.numpy as jnp
from jax import lax
from jax.experimental import pallas as pl
from jax.experimental.pallas import tpu as pltpu
from jax.sharding import PartitionSpec as P

EPSILON = 1e-06
F32 = jnp.float32
BF16 = jnp.bfloat16
VMEM_BYTES = 40 * 1024 * 1024


def split(x):
    high = x.astype(BF16)
    return high, (x - high.astype(F32)).astype(BF16)


def dot(a, b):
    return jnp.dot(a, b, preferred_element_type=F32)


def row_tile(rows):
    return next(size for size in (64, 32, 16, 8) if rows % size == 0)


def rows_at(first, count):
    return pl.ds(pl.multiple_of(first, count), count)


def start(copies):
    for copy in copies:
        copy.start()


def wait(copies):
    for copy in copies:
        copy.wait()


def load_blocks(src, dst, rows, sems):
    return [
        pltpu.make_async_copy(src.at[:, r, :], dst.at[pl.ds(r * rows, rows), :], sems.at[r])
        for r in range(src.shape[1])
    ]


def split_half(core, src, stacked):
    size, half = src.shape[0], stacked.shape[1]
    for side in range(2):

        @pl.when(core == side)
        def _():
            a, b = split(src[:, side * half : (side + 1) * half])
            stacked[0:size, :] = a
            stacked[size : 2 * size, :] = b
            stacked[2 * size : 3 * size, :] = a


def put_split(stacked, at, x):
    size = x.shape[1]
    a, b = split(x)
    stacked[at, 0:size] = a
    stacked[at, size : 2 * size] = a
    stacked[at, 2 * size : 3 * size] = b


def mix(operator, product, store):
    phys = len(operator)
    rows = product.shape[0] // phys
    tile = min(32, row_tile(rows))
    for first in range(0, rows, tile):
        pieces = [product[r * rows + first : r * rows + first + tile, :] for r in range(phys)]
        for p in range(phys):
            total = operator[p][0] * pieces[0]
            for r in range(1, phys):
                total = total + operator[p][r] * pieces[r]
            store(first, tile, p, *split(total))


def pick(refs, w, *at):
    count = refs[0].shape[0]
    low = jnp.minimum(w, count - 1)
    if len(refs) == 1:
        return refs[0][(low, *at)]
    high = jnp.maximum(w - count, 0)
    return jnp.where(w < count, refs[0][(low, *at)], refs[1][(high, *at)])


def run_pairs(number, phys, operators, pairs, sources, take, product, stacked, finish):
    def begin(i):
        take(i)
        product[...] = dot(sources[pairs[1, i]], stacked[...])

    def operator(i):
        w = pairs[0, i]
        return [[pick(operators, w, p, r) for r in range(phys)] for p in range(phys)]

    @pl.when(number > 0)
    def _():
        begin(0)

        @pl.loop(0, number - 1)
        def _(i):
            take(i + 1)
            store, close = finish(i)
            mix(operator(i), product, store)
            product[...] = dot(sources[pairs[1, i + 1]], stacked[...])
            close()

        store, close = finish(number - 1)
        mix(operator(number - 1), product, store)
        close()


def near_kernel(
    first_call, phys, chips, info, sizes, charges, operators, *refs,
):
    if first_call:
        energies, psi, left, right, total, share = refs[:6]
        raw, source, stacked, tall, product, mixed, pairs, sems, state = refs[6:]
    else:
        psi, left, right, base, total = refs[:5]
        raw, source, stacked, tall, product, mixed, pairs, sems = refs[5:]
    chip, core = info[0], info[1]
    sectors, size = psi.shape[0], psi.shape[1]
    count = left.shape[0]
    half = size // 2
    loads = []
    for t in range(sectors):
        loads += load_blocks(psi.at[t], raw.at[t], size, sems.at[t])
    start(loads)

    number = 0
    for w in range(count):
        for t in range(sectors):
            at = t - charges[w]
            inside = (at >= 0) & (at < sectors)
            pairs[0, number] = w
            pairs[1, number] = jnp.clip(at, 0, sectors - 1)
            pairs[2, number] = t
            number = number + inside.astype(jnp.int32)

    if not first_call:
        total[...] = base[...]
    tile = row_tile(size)
    for t in range(sectors):
        wait(loads[t * phys : (t + 1) * phys])
        limit = sizes[t]
        columns = lax.broadcasted_iota(jnp.int32, (tile, size), 1)
        lines = lax.broadcasted_iota(jnp.int32, (tile, size), 0)

        @pl.loop(0, size // tile)
        def _(i):
            keep = (columns < limit) & (lines + i * tile < limit)
            for r in range(phys):
                at = rows_at(r * size + i * tile, tile)
                x = jnp.where(keep, raw[t, at, :], 0)
                put_split(source.at[t], at, x)
                if first_call:
                    for side in range(2):

                        @pl.when(core == side)
                        def _():
                            state[t, rows_at(i * tile, tile), r * half : (r + 1) * half] = x[
                                :, side * half : (side + 1) * half
                            ]

            if first_call:
                at = rows_at(i * tile, tile)
                total[t, at, :] = state[t, at, :] * (energies[t] * (1.0 / chips))

    if first_call:
        rows = share.shape[2]
        for c in range(2):
            at = rows_at((2 * chip + (core ^ c)) * rows, rows)
            share[:, c] = state[:, at, :]

    def finish(i):
        w, t = pairs[0, i], pairs[2, i]

        def store(first, tile, p, a, b):
            cols = slice(p * half, (p + 1) * half)
            for place, value in enumerate((a, b, a)):
                mixed[place * size + first : place * size + first + tile, cols] = value

        def close():
            put_split(tall, slice(None), left[w, t])
            total[t] += dot(tall[...], mixed[...])

        return store, close

    def take(i):
        split_half(core, right.at[pairs[0, i], pairs[2, i]], stacked)

    run_pairs(number, phys, (operators,), pairs, source, take, product, stacked, finish)


def end_target(charge, sectors):
    return jnp.where(charge > 0, 0, sectors - 1)


def of_group(w, count, use):
    for group in range(2):

        @pl.when((w >= group * count) & (w < (group + 1) * count))
        def _():
            use(group, w - group * count)


def far_products(core, charges, operators, halo, right, raw, source, stacked, product, pairs, sems, finish):
    rows, phys, _ = halo[0].shape
    sectors = right[0].shape[1]
    count = charges[0].shape[0]
    loads = [load_blocks(halo[side], raw.at[side], rows, sems.at[side]) for side in range(2)]
    start(loads[0] + loads[1])
    number = 0
    for group in range(2):
        for w in range(count):
            charge = charges[group][w]
            pairs[0, number] = group * count + w
            pairs[1, number] = jnp.where(charge > 0, 0, 1)
            pairs[2, number] = end_target(charge, sectors)
            number = number + (charge != 0).astype(jnp.int32)
    lines = raw.shape[1]
    tile = row_tile(lines)
    for side in range(2):
        wait(loads[side])

        @pl.loop(0, lines // tile)
        def _(i):
            at = rows_at(i * tile, tile)
            put_split(source.at[side], at, raw[side, at, :])

    def take(i):
        t = pairs[2, i]
        of_group(pairs[0, i], count, lambda g, w: split_half(core, right[g].at[w, t], stacked))

    run_pairs(
        number, phys, operators, pairs, source, take, product, stacked,
        lambda i: (functools.partial(finish, pairs[0, i]), lambda: None),
    )
    return number


def far_first_kernel(
    info, charges_a, charges_b, operators_a, operators_b, low, high, right_a, right_b, early,
    raw, source, stacked, product, pairs, sems,
):
    half = low.shape[0]

    def store(w, first, tile, p, a, b):
        cols = slice(p * half, (p + 1) * half)
        early[w, 0, first : first + tile, cols] = a
        early[w, 1, first : first + tile, cols] = b

    far_products(
        info[1], (charges_a, charges_b), (operators_a, operators_b), (low, high), (right_a, right_b), raw,
        source, stacked, product, pairs, sems, store,
    )


def far_last_kernel(
    chips, info, charges_a, charges_b, operators_a, operators_b, low, high, right_a, right_b, left_a,
    left_b, near, early, *refs,
):
    outs = refs[:chips]
    raw, source, stacked, product, pairs, sems, tall, mixed, total = refs[chips:]
    chip, core = info[0], info[1]
    half = low.shape[0]
    size = 2 * half
    rows = outs[0].shape[2]
    count = charges_a.shape[0]

    def store(w, first, tile, p, a, b):
        cols = slice(p * half, (p + 1) * half)
        for place, value in enumerate((a, b, a)):
            at = rows_at(place * size + (1 - core) * half + first, tile)
            mixed[w, at, cols] = value

    number = far_products(
        core, (charges_a, charges_b), (operators_a, operators_b), (low, high), (right_a, right_b), raw,
        source, stacked, product, pairs, sems, store,
    )
    total[...] = near[...]

    @pl.loop(0, number)
    def _(i):
        w = pairs[0, i]
        t = pairs[2, i]
        for place, part in enumerate((0, 1, 0)):
            mixed[w, rows_at(place * size + core * half, half), :] = early[w, part]
        of_group(w, count, lambda g, v: put_split(tall, slice(None), (left_a, left_b)[g][v, t]))
        total[t] += dot(tall[...], mixed[w])

    for j in range(chips):
        for c in range(2):
            first = (2 * (chip ^ j) + (core ^ c)) * rows
            outs[j][:, c] = total[:, rows_at(first, rows), :]


def update_kernel(*refs):
    parts, (state, scale, mine, other, sums) = refs[:-5], refs[-5:]
    sectors, _, rows, lanes = state.shape
    tile = row_tile(rows)
    values = [jnp.zeros((8, lanes), F32)] * 5

    def fold(x):
        return jnp.sum(x.reshape(tile // 8, 8, lanes), axis=0)

    for t in range(sectors):
        for c in range(2):
            for first in range(0, rows, tile):
                at = (t, c, slice(first, first + tile), slice(None))
                total = parts[0][at]
                for part in parts[1:]:
                    total = total + part[at]
                s, k = state[at], scale[at]
                fixed = s - total * k
                slope = s * k
                (mine, other)[c][0, t, first : first + tile, :] = fixed
                (mine, other)[c][1, t, first : first + tile, :] = slope
                new = (s * total, s * s, fixed * fixed, fixed * slope, slope * slope)
                values = [v + fold(x) for v, x in zip(values, new)]
    column = lax.broadcasted_iota(jnp.int32, sums.shape, 1)
    result = jnp.zeros(sums.shape, F32)
    for i, v in enumerate(values):
        result = jnp.where(column == i, jnp.sum(v), result)
    sums[...] = result


def finish_kernel(numel, info, sums, mine, other, out, energies, whole, sems):
    core = info[1]
    column = lax.broadcasted_iota(jnp.int32, sums.shape, 1)
    values = [jnp.full((1, 128), jnp.sum(jnp.where(column == i, sums[...], 0)), F32) for i in range(5)]
    energy = values[0] / values[1]
    square = values[2] + 2 * energy * values[3] + energy * energy * values[4]
    factor = lax.rsqrt(jnp.maximum(square, 0) / numel + EPSILON)[0, 0]
    energy = energy[0, 0]
    energies[0] = energy
    _, sectors, rows, lanes = mine.shape
    phys = whole.shape[1]
    half = lanes // phys
    stores = []
    for t in range(sectors):
        for p in range(phys):
            cols = slice(p * half, (p + 1) * half)
            a = (mine[0, t, :, cols] + energy * mine[1, t, :, cols]) * factor
            b = (other[0, t, :, cols] + energy * other[1, t, :, cols]) * factor
            for side in range(2):

                @pl.when(core == side)
                def _():
                    whole[t, p, :, side * half : (side + 1) * half] = a
                    whole[t, p, :, (1 - side) * half : (2 - side) * half] = b

            copy = pltpu.make_async_copy(whole.at[t, p], out.at[t, :, p, :], sems.at[t, p])
            copy.start()
            stores.append(copy)
    wait(stores)


def swap_cores(x, count):
    return lax.ppermute(x, "term", [(i, i ^ 1) for i in range(count)])


def body(
    psi, precond, left_environment_block, right_env, term_operators, term_charge, sector_sizes,
    sector_energy,
):
    sectors, size, phys, _ = psi.shape
    terms = term_charge.shape[0]
    count, planes = lax.axis_size("term"), lax.axis_size("sector")
    chips = count // 2
    rows = size // count
    half = size // 2
    lanes = phys * half
    numel = sectors * planes * size * phys * size
    me = lax.axis_index("term")
    chip, core = me // 2, me % 2
    info = jnp.stack([chip, core]).astype(jnp.int32)

    positions = jnp.arange(size, dtype=jnp.int32)

    def edge(t):
        limit = sector_sizes[t]
        x = lax.dynamic_slice(psi, (t, core * half, 0, 0), (1, half, phys, size))[0]
        a = core * half + lax.broadcasted_iota(jnp.int32, x.shape, 0) < limit
        b = lax.broadcasted_iota(jnp.int32, x.shape, 2) < limit
        return jnp.where(a & b, x, 0)

    forward = [(i, i + 1) for i in range(planes - 1)]
    backward = [(b, a) for a, b in forward]
    low_a = lax.ppermute(edge(sectors - 1), "sector", forward)
    high_a = lax.ppermute(edge(0), "sector", backward)

    left_a, right_a, charges_a, operators_a = left_environment_block, right_env, term_charge, term_operators
    charges_b = swap_cores(charges_a, count)
    operators_b = swap_cores(operators_a, count)
    right_b = swap_cores(right_a, count)
    left_b = swap_cores(left_a, count)

    any_spec = pl.BlockSpec(memory_space=pl.ANY)
    smem = pl.BlockSpec(memory_space=pltpu.SMEM)
    vmem = pl.BlockSpec(memory_space=pltpu.VMEM)
    params = pltpu.CompilerParams(vmem_limit_bytes=VMEM_BYTES)
    wide = jax.ShapeDtypeStruct((sectors, size, lanes), F32)
    block = jax.ShapeDtypeStruct((sectors, 2, rows, lanes), F32)
    pair_list = pltpu.SMEM((3, 2 * terms * sectors + 1), jnp.int32)
    near_scratch = [
        pltpu.VMEM((sectors, phys * size, size), F32),
        pltpu.VMEM((sectors, phys * size, 3 * size), BF16),
        pltpu.VMEM((3 * size, half), BF16),
        pltpu.VMEM((size, 3 * size), BF16),
        pltpu.VMEM((phys * size, half), F32),
        pltpu.VMEM((3 * size, lanes), BF16),
        pair_list,
        pltpu.SemaphoreType.DMA((sectors, phys)),
    ]

    def cost(pairs):
        return pl.CostEstimate(
            flops=pairs * 3 * 4 * size * size * lanes, bytes_accessed=12 << 20, transcendentals=0
        )

    near, state = pl.pallas_call(
        functools.partial(near_kernel, True, phys, chips),
        out_shape=[wide, block],
        in_specs=[smem] * 5 + [any_spec] + [vmem] * 2,
        out_specs=[vmem] * 2,
        scratch_shapes=[*near_scratch, pltpu.VMEM((sectors, size, lanes), F32)],
        compiler_params=params,
        cost_estimate=cost(terms * sectors),
        name="near_own",
    )(info, sector_sizes, charges_a, operators_a, sector_energy, psi, left_a, right_a)
    near = pl.pallas_call(
        functools.partial(near_kernel, False, phys, chips),
        out_shape=wide,
        in_specs=[smem] * 4 + [any_spec] + [vmem] * 3,
        out_specs=vmem,
        scratch_shapes=near_scratch,
        compiler_params=params,
        cost_estimate=cost(terms * sectors),
        name="near_partner",
    )(info, sector_sizes, charges_b, operators_b, psi, left_b, right_b, near)

    low_a, high_a, near = lax.optimization_barrier((low_a, high_a, near))
    low_b = swap_cores(low_a, count)
    high_b = swap_cores(high_a, count)

    far_scratch = [
        pltpu.VMEM((2, phys * half, size), F32),
        pltpu.VMEM((2, phys * half, 3 * size), BF16),
        pltpu.VMEM((3 * size, half), BF16),
        pltpu.VMEM((phys * half, half), F32),
        pair_list,
        pltpu.SemaphoreType.DMA((2, phys)),
    ]
    early = pl.pallas_call(
        far_first_kernel,
        out_shape=jax.ShapeDtypeStruct((2 * terms, 2, half, lanes), BF16),
        in_specs=[smem] * 5 + [vmem] * 4,
        out_specs=vmem,
        scratch_shapes=far_scratch,
        compiler_params=params,
        cost_estimate=cost(terms // 2),
        name="far_first",
    )(info, charges_a, charges_b, operators_a, operators_b, low_a, high_a, right_a, right_b)

    parts = pl.pallas_call(
        functools.partial(far_last_kernel, chips),
        out_shape=[block] * chips,
        in_specs=[smem] * 5 + [vmem] * 8,
        out_specs=[vmem] * chips,
        scratch_shapes=[
            *far_scratch,
            pltpu.VMEM((size, 3 * size), BF16),
            pltpu.VMEM((2 * terms, 3 * size, lanes), BF16),
            pltpu.VMEM((sectors, size, lanes), F32),
        ],
        compiler_params=params,
        cost_estimate=cost(terms),
        name="far_last",
    )(
        info, charges_a, charges_b, operators_a, operators_b, low_b, high_b, right_a, right_b, left_a, left_b,
        near, early,
    )

    *parts, precond = lax.optimization_barrier((*parts, precond))
    parts = [parts[0]] + [
        lax.ppermute(parts[j], "term", [(i, i ^ (2 * j)) for i in range(count)]) for j in range(1, chips)
    ]

    first = chip * 2 * rows
    inside = positions[None, :] < sector_sizes[:, None]
    scale = lax.dynamic_slice(
        precond, (0, first, 0, core * half), (sectors, 2 * rows, phys, half)
    ).astype(F32)
    a = lax.dynamic_slice(inside, (0, first), (sectors, 2 * rows))
    b = lax.dynamic_slice(inside, (0, core * half), (sectors, half))
    scale = jnp.where(a[:, :, None, None] & b[:, None, None, :], 1.0 / scale, 0)
    scale = scale.reshape(sectors, 2, rows, lanes)
    scale = jnp.where(core == 0, scale, scale[:, ::-1])

    devices = count * planes
    pair = jax.ShapeDtypeStruct((2, sectors, rows, lanes), F32)
    mine, other, sums = pl.pallas_call(
        update_kernel,
        out_shape=[pair, pair, jax.ShapeDtypeStruct((devices, 128), F32)],
        in_specs=[vmem] * (chips + 2),
        out_specs=[vmem] * 3,
        compiler_params=params,
        name="update",
    )(*parts, state, scale)
    other = swap_cores(other, count)
    sums = lax.all_to_all(sums, ("sector", "term"), 0, 0, tiled=True)
    return tuple(
        pl.pallas_call(
            functools.partial(finish_kernel, numel),
            out_shape=[
                jax.ShapeDtypeStruct((sectors, rows, phys, size), F32),
                jax.ShapeDtypeStruct((1,), F32),
            ],
            in_specs=[smem] + [vmem] * 3,
            out_specs=[any_spec, smem],
            scratch_shapes=[
                pltpu.VMEM((sectors, phys, rows, size), F32),
                pltpu.SemaphoreType.DMA((sectors, phys)),
            ],
            compiler_params=params,
            name="finish",
        )(info, sums, mine, other)
    )


def solution(mesh):
    in_specs = (
        P("sector", None, None, None),
        P("sector", None, None, None),
        P("term", "sector", None, None),
        P("term", "sector", None, None),
        P("term", None, None),
        P("term"),
        P("sector"),
        P("sector"),
    )
    out_specs = (P("sector", "term", None, None), P())
    return jax.shard_map(body, mesh=mesh, in_specs=in_specs, out_specs=out_specs, check_vma=False)
```

```python
import functools

import jax
import jax.numpy as jnp
from jax import lax
from jax.experimental import pallas as pl
from jax.experimental.pallas import tpu as pltpu
from jax.sharding import PartitionSpec as P

EPSILON = 1e-06
F32 = jnp.float32
BF16 = jnp.bfloat16
VMEM_BYTES = 24 * 1024 * 1024
SEND_BYTES = 60 * 1024 * 1024


def split(x):
    high = x.astype(BF16)
    return high, (x - high.astype(F32)).astype(BF16)


def dot(a, b):
    return jnp.dot(a, b, preferred_element_type=F32)


def row_tile(rows):
    return next(size for size in (64, 32, 16, 8) if rows % size == 0)


class Window:
    def __init__(self, flat, offset, shape):
        self.flat, self.offset, self.shape = flat, offset, shape

    def __getitem__(self, at):
        place = 0
        for size, i in zip(self.shape, at if isinstance(at, tuple) else (at,)):
            place = place * size + i
        return self.flat[self.offset + place]


def unpack(ints, floats, sectors, terms, phys):
    return (
        Window(ints, 2 + sectors, (terms,)),
        Window(floats, 0, (terms, phys, phys)),
        Window(ints, 2, (sectors,)),
        Window(floats, terms * phys * phys, (sectors,)),
    )


def rows_at(first, count):
    return pl.ds(pl.multiple_of(first, count), count)


def start(copies):
    for copy in copies:
        copy.start()


def wait(copies):
    for copy in copies:
        copy.wait()


def load_blocks(src, dst, rows, sems):
    return [
        pltpu.make_async_copy(src.at[:, r, :], dst.at[pl.ds(r * rows, rows), :], sems.at[r])
        for r in range(src.shape[1])
    ]


def split_half(core, src, stacked):
    size, half = src.shape[0], stacked.shape[1]
    for side in range(2):

        @pl.when(core == side)
        def _():
            a, b = split(src[:, side * half : (side + 1) * half])
            stacked[0:size, :] = a
            stacked[size : 2 * size, :] = b
            stacked[2 * size : 3 * size, :] = a


def put_split(stacked, at, x):
    size = x.shape[1]
    a, b = split(x)
    stacked[at, 0:size] = a
    stacked[at, size : 2 * size] = a
    stacked[at, 2 * size : 3 * size] = b


def mix(operator, product, store):
    phys = len(operator)
    rows = product.shape[0] // phys
    tile = min(32, row_tile(rows))
    for first in range(0, rows, tile):
        pieces = [product[r * rows + first : r * rows + first + tile, :] for r in range(phys)]
        for p in range(phys):
            total = operator[p][0] * pieces[0]
            for r in range(1, phys):
                total = total + operator[p][r] * pieces[r]
            store(first, tile, p, *split(total))


def pick(refs, w, *at):
    count = refs[0].shape[0]
    low = jnp.minimum(w, count - 1)
    if len(refs) == 1:
        return refs[0][(low, *at)]
    high = jnp.maximum(w - count, 0)
    return jnp.where(w < count, refs[0][(low, *at)], refs[1][(high, *at)])


def run_pairs(number, phys, operators, pairs, sources, take, product, stacked, finish):
    def begin(i):
        take(i)
        product[...] = dot(sources[pairs[1, i]], stacked[...])

    def operator(i):
        w = pairs[0, i]
        return [[pick(operators, w, p, r) for r in range(phys)] for p in range(phys)]

    @pl.when(number > 0)
    def _():
        begin(0)

        @pl.loop(0, number - 1)
        def _(i):
            take(i + 1)
            store, close = finish(i)
            mix(operator(i), product, store)
            product[...] = dot(sources[pairs[1, i + 1]], stacked[...])
            close()

        store, close = finish(number - 1)
        mix(operator(number - 1), product, store)
        close()


def load_states(sizes, loads, raw, source):
    sectors, lines, size = raw.shape
    phys = lines // size
    tile = row_tile(size)
    columns = lax.broadcasted_iota(jnp.int32, (tile, size), 1)
    rows = lax.broadcasted_iota(jnp.int32, (tile, size), 0)
    for t in range(sectors):
        wait(loads[t * phys : (t + 1) * phys])

        @pl.loop(0, size // tile)
        def _(i):
            keep = (columns < sizes[t]) & (rows + i * tile < sizes[t])
            for r in range(phys):
                at = rows_at(r * size + i * tile, tile)
                put_split(source.at[t], at, jnp.where(keep, raw[t, at, :], 0))


def store_share(sizes, chip, core, raw, share):
    sectors, _, rows, lanes = share.shape
    size = raw.shape[2]
    half = size // 2
    phys = lanes // half
    columns = lax.broadcasted_iota(jnp.int32, (rows, half), 1)
    lines = lax.broadcasted_iota(jnp.int32, (rows, half), 0)
    for c in range(2):
        first = (2 * chip + (core ^ c)) * rows
        for side in range(2):

            @pl.when(core == side)
            def _():
                for t in range(sectors):
                    keep = (columns + side * half < sizes[t]) & (lines + first < sizes[t])
                    for r in range(phys):
                        x = raw[t, rows_at(r * size + first, rows), side * half : (side + 1) * half]
                        share[t, c, :, r * half : (r + 1) * half] = jnp.where(keep, x, 0)


def near_kernel(
    first_call, phys, info, ints, floats, *refs,
):
    if first_call:
        psi, left, right, total, share, source = refs[:6]
        stacked, tall, product, mixed, pairs, raw, sems = refs[6:]
    else:
        source, left, right, base, total = refs[:5]
        stacked, tall, product, mixed, pairs = refs[5:]
    chip, core = info[0], info[1]
    sectors, size = left.shape[1], left.shape[2]
    count = left.shape[0]
    half = size // 2
    charges, operators, sizes, _ = unpack(ints, floats, sectors, count, phys)
    if first_call:
        loads = []
        for t in range(sectors):
            loads += load_blocks(psi.at[t], raw.at[t], size, sems.at[t])
        start(loads)

    number = 0
    for w in range(count):
        for t in range(sectors):
            at = t - charges[w]
            inside = (at >= 0) & (at < sectors)
            pairs[0, number] = w
            pairs[1, number] = jnp.clip(at, 0, sectors - 1)
            pairs[2, number] = t
            number = number + inside.astype(jnp.int32)

    if first_call:
        load_states(sizes, loads, raw, source)
        store_share(sizes, chip, core, raw, share)
        total[...] = jnp.zeros_like(total)
    else:
        total[...] = base[...]

    def finish(i):
        w, t = pairs[0, i], pairs[2, i]

        def store(first, tile, p, a, b):
            cols = slice(p * half, (p + 1) * half)
            for place, value in enumerate((a, b, a)):
                mixed[place * size + first : place * size + first + tile, cols] = value

        def close():
            put_split(tall, slice(None), left[w, t])
            total[t] += dot(tall[...], mixed[...])

        return store, close

    def take(i):
        split_half(core, right.at[pairs[0, i], pairs[2, i]], stacked)

    run_pairs(number, phys, (operators,), pairs, source, take, product, stacked, finish)


def end_target(charge, sectors):
    return jnp.where(charge > 0, 0, sectors - 1)


def of_group(w, count, use):
    for group in range(2):

        @pl.when((w >= group * count) & (w < (group + 1) * count))
        def _():
            use(group, w - group * count)


def put_columns(core, src, stacked):
    half = src.shape[1] // 2
    for side in range(2):

        @pl.when(core == side)
        def _():
            put_split(stacked, slice(None), src[:, side * half : (side + 1) * half])


def far_kernel(
    last, chips, info, ints_a, ints_b, floats_a, floats_b, low, high, right_a, right_b, left_a,
    left_b, base, *refs,
):
    if last:
        many = chips * base.shape[0]
        outs = refs[:many]
        source, stacked, product, tall, mixed, pairs, total = refs[many:]
    else:
        total, source, stacked, product, tall, mixed, pairs = refs
    chip, core = info[0], info[1]
    part = 1 - core if last else core
    rights, lefts = (right_a, right_b), (left_a, left_b)
    lines = low.shape[0]
    half = stacked.shape[1]
    phys = lines // half
    count, sectors = left_a.shape[:2]
    views = [
        unpack(a, b, sectors, count, phys) for a, b in ((ints_a, floats_a), (ints_b, floats_b))
    ]
    charges, operators = [v[0] for v in views], [v[1] for v in views]
    number = 0
    for group in range(2):
        for w in range(count):
            charge = charges[group][w]
            pairs[0, number] = group * count + w
            pairs[1, number] = jnp.where(charge > 0, 0, 1)
            pairs[2, number] = end_target(charge, sectors)
            number = number + (charge != 0).astype(jnp.int32)
    tile = row_tile(lines)
    for side, halo in enumerate((low, high)):

        @pl.loop(0, lines // tile)
        def _(i):
            at = rows_at(i * tile, tile)
            put_split(source.at[side], at, halo[at, :])

    total[...] = base[...]

    def take(i):
        t = pairs[2, i]
        of_group(pairs[0, i], count, lambda g, w: split_half(core, rights[g].at[w, t], stacked))

    def finish(i):
        t = pairs[2, i]
        of_group(pairs[0, i], count, lambda g, w: put_columns(part, lefts[g].at[w, t], tall))

        def store(first, rows, p, a, b):
            cols = slice(p * half, (p + 1) * half)
            for place, value in enumerate((a, b, a)):
                mixed[place * half + first : place * half + first + rows, cols] = value

        def close():
            total[t] += dot(tall[...], mixed[...])

        return store, close

    run_pairs(number, phys, operators, pairs, source, take, product, stacked, finish)
    if last:
        rows = outs[0].shape[1]
        for j in range(chips):
            for c in range(2):
                first = (2 * (chip ^ j) + (core ^ c)) * rows
                for t in range(sectors):
                    outs[j * sectors + t][c] = total[t, rows_at(first, rows), :]


def send_kernel(info, ints, psi, up, down, sems):
    sectors, size, phys, _ = psi.shape
    half = size // 2
    sizes = Window(ints, 2, (sectors,))
    first = info[1] * half
    work = ((sectors - 1, up), (0, down))
    loads = [
        load_blocks(psi.at[t, rows_at(first, half)], out, half, sems.at[side])
        for side, (t, out) in enumerate(work)
    ]
    start(loads[0] + loads[1])
    tile = row_tile(half)
    columns = lax.broadcasted_iota(jnp.int32, (tile, size), 1)
    rows = lax.broadcasted_iota(jnp.int32, (tile, size), 0)
    for side, (t, out) in enumerate(work):
        wait(loads[side])

        @pl.loop(0, half // tile)
        def _(i):
            keep = (columns < sizes[t]) & (rows + (first + i * tile) < sizes[t])
            for r in range(phys):
                at = rows_at(r * half + i * tile, tile)
                out[at, :] = jnp.where(keep, out[at, :], 0)


def update_kernel(phys, terms, floats, *refs):
    parts, (state, scale, mine, other, sums) = refs[:-5], refs[-5:]
    sectors, _, rows, lanes = state.shape
    tile = row_tile(rows)
    values = [jnp.zeros((8, lanes), F32)] * 5
    energies = Window(floats, terms * phys * phys, (sectors,))
    count = len(parts) // sectors

    def fold(x):
        return jnp.sum(x.reshape(tile // 8, 8, lanes), axis=0)

    for t in range(sectors):
        for c in range(2):
            for first in range(0, rows, tile):
                at = (t, c, slice(first, first + tile), slice(None))
                s, k = state[at], scale[at]
                total = energies[t] * s
                for part in parts[t * count : (t + 1) * count]:
                    total = total + part[at[1:]]
                fixed = s - total * k
                slope = s * k
                (mine, other)[c][0, t, first : first + tile, :] = fixed
                (mine, other)[c][1, t, first : first + tile, :] = slope
                new = (s * total, s * s, fixed * fixed, fixed * slope, slope * slope)
                values = [v + fold(x) for v, x in zip(values, new)]
    column = lax.broadcasted_iota(jnp.int32, sums.shape, 1)
    result = jnp.zeros(sums.shape, F32)
    for i, v in enumerate(values):
        result = jnp.where(column == i, jnp.sum(v), result)
    sums[...] = result


def finish_kernel(numel, info, sums, mine, other, out, energies, whole, sems):
    core = info[1]
    column = lax.broadcasted_iota(jnp.int32, sums.shape, 1)
    values = [jnp.full((1, 128), jnp.sum(jnp.where(column == i, sums[...], 0)), F32) for i in range(5)]
    energy = values[0] / values[1]
    square = values[2] + 2 * energy * values[3] + energy * energy * values[4]
    factor = lax.rsqrt(jnp.maximum(square, 0) / numel + EPSILON)[0, 0]
    energy = energy[0, 0]
    energies[0] = energy
    _, sectors, rows, lanes = mine.shape
    phys = whole.shape[1]
    half = lanes // phys
    stores = []
    for t in range(sectors):
        for p in range(phys):
            cols = slice(p * half, (p + 1) * half)
            a = (mine[0, t, :, cols] + energy * mine[1, t, :, cols]) * factor
            b = (other[0, t, :, cols] + energy * other[1, t, :, cols]) * factor
            for side in range(2):

                @pl.when(core == side)
                def _():
                    whole[t, p, :, side * half : (side + 1) * half] = a
                    whole[t, p, :, (1 - side) * half : (2 - side) * half] = b

            copy = pltpu.make_async_copy(whole.at[t, p], out.at[t, :, p, :], sems.at[t, p])
            copy.start()
            stores.append(copy)
    wait(stores)


def swap_cores(x, count):
    return lax.ppermute(x, "term", [(i, i ^ 1) for i in range(count)])


def sum_chips(parts, count, backward):
    chips = len(parts)
    bits = [1 << i for i in range(chips.bit_length() - 1)]
    if backward:
        bits.reverse()
    parts = dict(enumerate(parts))
    arrived = [parts[0]]
    for step, bit in enumerate(bits):
        going = [j for j in parts if j & bit]
        later = sum(bits[step + 1 :])
        for j in sorted(going, key=lambda j: not (j & later)):
            part = lax.ppermute(parts.pop(j), "term", [(i, i ^ (2 * bit)) for i in range(count)])
            if j == bit:
                arrived.append(part)
            else:
                parts[j ^ bit] = parts[j ^ bit] + part
    return arrived


def body(
    psi, precond, left_environment_block, right_env, term_operators, term_charge, sector_sizes,
    sector_energy,
):
    sectors, size, phys, _ = psi.shape
    terms = term_charge.shape[0]
    count, planes = lax.axis_size("term"), lax.axis_size("sector")
    chips = count // 2
    rows = size // count
    half = size // 2
    lanes = phys * half
    numel = sectors * planes * size * phys * size
    me = lax.axis_index("term")
    chip, core = me // 2, me % 2
    info = jnp.concatenate([jnp.stack([chip, core]).astype(jnp.int32), sector_sizes, term_charge])
    ints_a = info
    floats_a = jnp.concatenate([term_operators.reshape(-1), sector_energy])

    positions = jnp.arange(size, dtype=jnp.int32)

    any_spec = pl.BlockSpec(memory_space=pl.ANY)
    smem = pl.BlockSpec(memory_space=pltpu.SMEM)
    vmem = pl.BlockSpec(memory_space=pltpu.VMEM)
    params = pltpu.CompilerParams(vmem_limit_bytes=VMEM_BYTES)

    edge = jax.ShapeDtypeStruct((phys * half, size), F32)
    up, down = pl.pallas_call(
        send_kernel,
        out_shape=[edge] * 2,
        in_specs=[smem] * 2 + [any_spec],
        out_specs=[vmem] * 2,
        scratch_shapes=[pltpu.SemaphoreType.DMA((2, phys))],
        compiler_params=pltpu.CompilerParams(vmem_limit_bytes=SEND_BYTES),
        name="send",
    )(info, ints_a, psi)
    forward = [(i, i + 1) for i in range(planes - 1)]
    backward = [(b, a) for a, b in forward]
    low_a = lax.ppermute(up, "sector", forward)
    high_a = lax.ppermute(down, "sector", backward)

    left_a, right_a = left_environment_block, right_env
    ints_b = swap_cores(ints_a, count)
    floats_b = swap_cores(floats_a, count)
    right_b = swap_cores(right_a, count)
    left_b = swap_cores(left_a, count)

    wide = jax.ShapeDtypeStruct((sectors, size, lanes), F32)
    block = jax.ShapeDtypeStruct((sectors, 2, rows, lanes), F32)
    piece = jax.ShapeDtypeStruct((2, rows, lanes), F32)
    pair_list = pltpu.SMEM((3, 2 * terms * sectors + 1), jnp.int32)
    splits = (sectors, phys * size, 3 * size)
    near_scratch = [
        pltpu.VMEM((3 * size, half), BF16),
        pltpu.VMEM((size, 3 * size), BF16),
        pltpu.VMEM((phys * size, half), F32),
        pltpu.VMEM((3 * size, lanes), BF16),
        pair_list,
    ]

    def cost(pairs):
        return pl.CostEstimate(
            flops=pairs * 3 * 4 * size * size * lanes, bytes_accessed=12 << 20, transcendentals=0
        )

    near, state, source = pl.pallas_call(
        functools.partial(near_kernel, True, phys),
        out_shape=[wide, block, jax.ShapeDtypeStruct(splits, BF16)],
        in_specs=[smem] * 3 + [any_spec] + [vmem] * 2,
        out_specs=[vmem] * 3,
        scratch_shapes=[
            *near_scratch,
            pltpu.VMEM((sectors, phys * size, size), F32),
            pltpu.SemaphoreType.DMA((sectors, phys)),
        ],
        compiler_params=params,
        cost_estimate=cost(terms * sectors),
        name="near_own",
    )(info, ints_a, floats_a, psi, left_a, right_a)
    near = pl.pallas_call(
        functools.partial(near_kernel, False, phys),
        out_shape=wide,
        in_specs=[smem] * 3 + [vmem] * 4,
        out_specs=vmem,
        scratch_shapes=near_scratch,
        compiler_params=params,
        cost_estimate=cost(terms * sectors),
        name="near_partner",
    )(info, ints_b, floats_b, source, left_b, right_b, near)

    low_a, high_a, near = lax.optimization_barrier((low_a, high_a, near))
    low_b = swap_cores(low_a, count)
    high_b = swap_cores(high_a, count)

    def far(last, low, high, base):
        return pl.pallas_call(
            functools.partial(far_kernel, last, chips),
            out_shape=[piece] * (chips * sectors) if last else wide,
            in_specs=[smem] * 5 + [vmem] * 7,
            out_specs=[vmem] * (chips * sectors) if last else vmem,
            scratch_shapes=[
                pltpu.VMEM((2, phys * half, 3 * size), BF16),
                pltpu.VMEM((3 * size, half), BF16),
                pltpu.VMEM((phys * half, half), F32),
                pltpu.VMEM((size, 3 * half), BF16),
                pltpu.VMEM((3 * half, lanes), BF16),
                pair_list,
            ]
            + [pltpu.VMEM((sectors, size, lanes), F32)] * last,
            compiler_params=params,
            cost_estimate=cost(terms // 2),
            name="far_last" if last else "far_first",
        )(
            info, ints_a, ints_b, floats_a, floats_b, low, high, right_a, right_b, left_a, left_b,
            base,
        )

    parts = far(True, low_b, high_b, far(False, low_a, high_a, near))

    *parts, precond, sector_sizes = lax.optimization_barrier((*parts, precond, sector_sizes))
    parts = [sum_chips(parts[t::sectors], count, t % 2 == 1) for t in range(sectors)]

    first = chip * 2 * rows
    inside = positions[None, :] < sector_sizes[:, None]
    scale = lax.dynamic_slice(
        precond, (0, first, 0, core * half), (sectors, 2 * rows, phys, half)
    ).astype(F32)
    a = lax.dynamic_slice(inside, (0, first), (sectors, 2 * rows))
    b = lax.dynamic_slice(inside, (0, core * half), (sectors, half))
    scale = jnp.where(a[:, :, None, None] & b[:, None, None, :], 1.0 / scale, 0)
    scale = scale.reshape(sectors, 2, rows, lanes)
    scale = jnp.where(core == 0, scale, scale[:, ::-1])

    devices = count * planes
    pair = jax.ShapeDtypeStruct((2, sectors, rows, lanes), F32)
    mine, other, sums = pl.pallas_call(
        functools.partial(update_kernel, phys, terms),
        out_shape=[pair, pair, jax.ShapeDtypeStruct((devices, 128), F32)],
        in_specs=[smem] + [vmem] * (sum(map(len, parts)) + 2),
        out_specs=[vmem] * 3,
        compiler_params=params,
        name="update",
    )(floats_a, *sum(parts, []), state, scale)
    other = swap_cores(other, count)
    sums = lax.all_to_all(sums, ("sector", "term"), 0, 0, tiled=True)
    return tuple(
        pl.pallas_call(
            functools.partial(finish_kernel, numel),
            out_shape=[
                jax.ShapeDtypeStruct((sectors, rows, phys, size), F32),
                jax.ShapeDtypeStruct((1,), F32),
            ],
            in_specs=[smem] + [vmem] * 3,
            out_specs=[any_spec, smem],
            scratch_shapes=[
                pltpu.VMEM((sectors, phys, rows, size), F32),
                pltpu.SemaphoreType.DMA((sectors, phys)),
            ],
            compiler_params=params,
            name="finish",
        )(info, sums, mine, other)
    )


def solution(mesh):
    in_specs = (
        P("sector", None, None, None),
        P("sector", None, None, None),
        P("term", "sector", None, None),
        P("term", "sector", None, None),
        P("term", None, None),
        P("term"),
        P("sector"),
        P("sector"),
    )
    out_specs = (P("sector", "term", None, None), P())
    return jax.shard_map(body, mesh=mesh, in_specs=in_specs, out_specs=out_specs, check_vma=False)
```

```python
import functools

import jax
import jax.numpy as jnp
from jax import lax
from jax.experimental import pallas as pl
from jax.experimental.pallas import tpu as pltpu
from jax.sharding import PartitionSpec as P

EPSILON = 1e-06
F32 = jnp.float32
BF16 = jnp.bfloat16
VMEM_BYTES = 24 * 1024 * 1024
SEND_BYTES = 60 * 1024 * 1024


def split(x):
    high = x.astype(BF16)
    return high, (x - high.astype(F32)).astype(BF16)


def dot(a, b):
    return jnp.dot(a, b, preferred_element_type=F32)


def row_tile(rows):
    return next(size for size in (64, 32, 16, 8) if rows % size == 0)


class Window:
    def __init__(self, flat, offset, shape):
        self.flat, self.offset, self.shape = flat, offset, shape

    def __getitem__(self, at):
        place = 0
        for size, i in zip(self.shape, at if isinstance(at, tuple) else (at,)):
            place = place * size + i
        return self.flat[self.offset + place]


def unpack(ints, floats, sectors, terms, phys):
    return (
        Window(ints, 2 + sectors, (terms,)),
        Window(floats, 0, (terms, phys, phys)),
        Window(ints, 2, (sectors,)),
        Window(floats, terms * phys * phys, (sectors,)),
    )


def rows_at(first, count):
    return pl.ds(pl.multiple_of(first, count), count)


def start(copies):
    for copy in copies:
        copy.start()


def wait(copies):
    for copy in copies:
        copy.wait()


def load_blocks(src, dst, rows, sems):
    return [
        pltpu.make_async_copy(src.at[:, r, :], dst.at[pl.ds(r * rows, rows), :], sems.at[r])
        for r in range(src.shape[1])
    ]


def split_half(core, src, stacked):
    size, half = src.shape[0], stacked.shape[1]
    for side in range(2):

        @pl.when(core == side)
        def _():
            a, b = split(src[:, side * half : (side + 1) * half])
            stacked[0:size, :] = a
            stacked[size : 2 * size, :] = b
            stacked[2 * size : 3 * size, :] = a


def put_split(stacked, at, x):
    size = x.shape[1]
    a, b = split(x)
    stacked[at, 0:size] = a
    stacked[at, size : 2 * size] = a
    stacked[at, 2 * size : 3 * size] = b


def mix(operator, product, store):
    phys = len(operator)
    rows = product.shape[0] // phys
    tile = min(32, row_tile(rows))
    for first in range(0, rows, tile):
        pieces = [product[r * rows + first : r * rows + first + tile, :] for r in range(phys)]
        for p in range(phys):
            total = operator[p][0] * pieces[0]
            for r in range(1, phys):
                total = total + operator[p][r] * pieces[r]
            store(first, tile, p, *split(total))


def pick(refs, w, *at):
    count = refs[0].shape[0]
    low = jnp.minimum(w, count - 1)
    if len(refs) == 1:
        return refs[0][(low, *at)]
    high = jnp.maximum(w - count, 0)
    return jnp.where(w < count, refs[0][(low, *at)], refs[1][(high, *at)])


def run_pairs(number, phys, operators, pairs, sources, take, product, stacked, finish):
    def begin(i):
        take(i)
        product[...] = dot(sources[pairs[1, i]], stacked[...])

    def operator(i):
        w = pairs[0, i]
        return [[pick(operators, w, p, r) for r in range(phys)] for p in range(phys)]

    @pl.when(number > 0)
    def _():
        begin(0)

        @pl.loop(0, number - 1)
        def _(i):
            take(i + 1)
            store, close = finish(i)
            mix(operator(i), product, store)
            product[...] = dot(sources[pairs[1, i + 1]], stacked[...])
            close()

        store, close = finish(number - 1)
        mix(operator(number - 1), product, store)
        close()


def load_states(sizes, loads, raw, source):
    sectors, lines, size = raw.shape
    phys = lines // size
    tile = row_tile(size)
    columns = lax.broadcasted_iota(jnp.int32, (tile, size), 1)
    rows = lax.broadcasted_iota(jnp.int32, (tile, size), 0)
    for t in range(sectors):
        wait(loads[t * phys : (t + 1) * phys])

        @pl.loop(0, size // tile)
        def _(i):
            keep = (columns < sizes[t]) & (rows + i * tile < sizes[t])
            for r in range(phys):
                at = rows_at(r * size + i * tile, tile)
                put_split(source.at[t], at, jnp.where(keep, raw[t, at, :], 0))


def store_share(sizes, chip, core, raw, share):
    sectors, _, rows, lanes = share.shape
    size = raw.shape[2]
    half = size // 2
    phys = lanes // half
    columns = lax.broadcasted_iota(jnp.int32, (rows, half), 1)
    lines = lax.broadcasted_iota(jnp.int32, (rows, half), 0)
    for c in range(2):
        first = (2 * chip + (core ^ c)) * rows
        for side in range(2):

            @pl.when(core == side)
            def _():
                for t in range(sectors):
                    keep = (columns + side * half < sizes[t]) & (lines + first < sizes[t])
                    for r in range(phys):
                        x = raw[t, rows_at(r * size + first, rows), side * half : (side + 1) * half]
                        share[t, c, :, r * half : (r + 1) * half] = jnp.where(keep, x, 0)


def near_kernel(
    first_call, phys, info, ints, floats, *refs,
):
    if first_call:
        psi, left, right, total, share, source = refs[:6]
        stacked, tall, product, mixed, pairs, raw, sems = refs[6:]
    else:
        source, left, right, base, total = refs[:5]
        stacked, tall, product, mixed, pairs = refs[5:]
    chip, core = info[0], info[1]
    sectors, size = left.shape[1], left.shape[2]
    count = left.shape[0]
    half = size // 2
    charges, operators, sizes, _ = unpack(ints, floats, sectors, count, phys)
    if first_call:
        loads = []
        for t in range(sectors):
            loads += load_blocks(psi.at[t], raw.at[t], size, sems.at[t])
        start(loads)

    number = 0
    for w in range(count):
        for t in range(sectors):
            at = t - charges[w]
            inside = (at >= 0) & (at < sectors)
            pairs[0, number] = w
            pairs[1, number] = jnp.clip(at, 0, sectors - 1)
            pairs[2, number] = t
            number = number + inside.astype(jnp.int32)

    if first_call:
        load_states(sizes, loads, raw, source)
        store_share(sizes, chip, core, raw, share)
        total[...] = jnp.zeros_like(total)
    else:
        total[...] = base[...]

    def finish(i):
        w, t = pairs[0, i], pairs[2, i]

        def store(first, tile, p, a, b):
            cols = slice(p * half, (p + 1) * half)
            for place, value in enumerate((a, b, a)):
                mixed[place * size + first : place * size + first + tile, cols] = value

        def close():
            put_split(tall, slice(None), left[w, t])
            total[t] += dot(tall[...], mixed[...])

        return store, close

    def take(i):
        split_half(core, right.at[pairs[0, i], pairs[2, i]], stacked)

    run_pairs(number, phys, (operators,), pairs, source, take, product, stacked, finish)


def end_target(charge, sectors):
    return jnp.where(charge > 0, 0, sectors - 1)


def of_group(w, count, use):
    for group in range(2):

        @pl.when((w >= group * count) & (w < (group + 1) * count))
        def _():
            use(group, w - group * count)


def put_columns(core, src, stacked):
    half = src.shape[1] // 2
    for side in range(2):

        @pl.when(core == side)
        def _():
            put_split(stacked, slice(None), src[:, side * half : (side + 1) * half])


def far_kernel(
    last, chips, info, ints_a, ints_b, floats_a, floats_b, low, high, right_a, right_b, left_a,
    left_b, base, *refs,
):
    if last:
        many = chips * base.shape[0]
        outs = refs[:many]
        source, stacked, product, tall, mixed, pairs, total = refs[many:]
    else:
        total, source, stacked, product, tall, mixed, pairs = refs
    chip, core = info[0], info[1]
    part = 1 - core if last else core
    rights, lefts = (right_a, right_b), (left_a, left_b)
    lines = low.shape[0]
    half = stacked.shape[1]
    phys = lines // half
    count, sectors = left_a.shape[:2]
    views = [
        unpack(a, b, sectors, count, phys) for a, b in ((ints_a, floats_a), (ints_b, floats_b))
    ]
    charges, operators = [v[0] for v in views], [v[1] for v in views]
    number = 0
    for group in range(2):
        for w in range(count):
            charge = charges[group][w]
            pairs[0, number] = group * count + w
            pairs[1, number] = jnp.where(charge > 0, 0, 1)
            pairs[2, number] = end_target(charge, sectors)
            number = number + (charge != 0).astype(jnp.int32)
    tile = row_tile(lines)
    for side, halo in enumerate((low, high)):

        @pl.loop(0, lines // tile)
        def _(i):
            at = rows_at(i * tile, tile)
            put_split(source.at[side], at, halo[at, :])

    total[...] = base[...]

    def take(i):
        t = pairs[2, i]
        of_group(pairs[0, i], count, lambda g, w: split_half(core, rights[g].at[w, t], stacked))

    def finish(i):
        t = pairs[2, i]
        of_group(pairs[0, i], count, lambda g, w: put_columns(part, lefts[g].at[w, t], tall))

        def store(first, rows, p, a, b):
            cols = slice(p * half, (p + 1) * half)
            for place, value in enumerate((a, b, a)):
                mixed[place * half + first : place * half + first + rows, cols] = value

        def close():
            total[t] += dot(tall[...], mixed[...])

        return store, close

    run_pairs(number, phys, operators, pairs, source, take, product, stacked, finish)
    if last:
        rows = outs[0].shape[1]
        for j in range(chips):
            for c in range(2):
                first = (2 * (chip ^ j) + (core ^ c)) * rows
                for t in range(sectors):
                    outs[j * sectors + t][c] = total[t, rows_at(first, rows), :]


def send_kernel(sizes, psi, up, down, sems):
    sectors, size, phys, _ = psi.shape
    half = size // 2
    first = lax.rem(lax.axis_index("term"), 2) * half
    work = ((sectors - 1, up), (0, down))
    loads = [
        load_blocks(psi.at[t, rows_at(first, half)], out, half, sems.at[side])
        for side, (t, out) in enumerate(work)
    ]
    start(loads[0] + loads[1])
    tile = row_tile(half)
    columns = lax.broadcasted_iota(jnp.int32, (tile, size), 1)
    rows = lax.broadcasted_iota(jnp.int32, (tile, size), 0)
    for side, (t, out) in enumerate(work):
        wait(loads[side])

        @pl.loop(0, half // tile)
        def _(i):
            keep = (columns < sizes[t]) & (rows + (first + i * tile) < sizes[t])
            for r in range(phys):
                at = rows_at(r * half + i * tile, tile)
                out[at, :] = jnp.where(keep, out[at, :], 0)


def update_kernel(phys, terms, floats, *refs):
    parts, (state, scale, mine, other, sums) = refs[:-5], refs[-5:]
    sectors, _, rows, lanes = state.shape
    tile = row_tile(rows)
    values = [jnp.zeros((8, lanes), F32)] * 5
    energies = Window(floats, terms * phys * phys, (sectors,))
    count = len(parts) // sectors

    def fold(x):
        return jnp.sum(x.reshape(tile // 8, 8, lanes), axis=0)

    for t in range(sectors):
        for c in range(2):
            for first in range(0, rows, tile):
                at = (t, c, slice(first, first + tile), slice(None))
                s, k = state[at], scale[at]
                total = energies[t] * s
                for part in parts[t * count : (t + 1) * count]:
                    total = total + part[at[1:]]
                fixed = s - total * k
                slope = s * k
                (mine, other)[c][0, t, first : first + tile, :] = fixed
                (mine, other)[c][1, t, first : first + tile, :] = slope
                new = (s * total, s * s, fixed * fixed, fixed * slope, slope * slope)
                values = [v + fold(x) for v, x in zip(values, new)]
    column = lax.broadcasted_iota(jnp.int32, sums.shape, 1)
    result = jnp.zeros(sums.shape, F32)
    for i, v in enumerate(values):
        result = jnp.where(column == i, jnp.sum(v), result)
    sums[...] = result


def finish_kernel(numel, info, sums, mine, other, out, energies, whole, sems):
    core = info[1]
    column = lax.broadcasted_iota(jnp.int32, sums.shape, 1)
    values = [jnp.full((1, 128), jnp.sum(jnp.where(column == i, sums[...], 0)), F32) for i in range(5)]
    energy = values[0] / values[1]
    square = values[2] + 2 * energy * values[3] + energy * energy * values[4]
    factor = lax.rsqrt(jnp.maximum(square, 0) / numel + EPSILON)[0, 0]
    energy = energy[0, 0]
    energies[0] = energy
    _, sectors, rows, lanes = mine.shape
    phys = whole.shape[1]
    half = lanes // phys
    stores = []
    for t in range(sectors):
        for p in range(phys):
            cols = slice(p * half, (p + 1) * half)
            a = (mine[0, t, :, cols] + energy * mine[1, t, :, cols]) * factor
            b = (other[0, t, :, cols] + energy * other[1, t, :, cols]) * factor
            for side in range(2):

                @pl.when(core == side)
                def _():
                    whole[t, p, :, side * half : (side + 1) * half] = a
                    whole[t, p, :, (1 - side) * half : (2 - side) * half] = b

            copy = pltpu.make_async_copy(whole.at[t, p], out.at[t, :, p, :], sems.at[t, p])
            copy.start()
            stores.append(copy)
    wait(stores)


def swap_cores(x, count):
    return lax.ppermute(x, "term", [(i, i ^ 1) for i in range(count)])


def sum_chips(parts, count, backward):
    chips = len(parts)
    bits = [1 << i for i in range(chips.bit_length() - 1)]
    if backward:
        bits.reverse()
    parts = dict(enumerate(parts))
    arrived = [parts[0]]
    for step, bit in enumerate(bits):
        going = [j for j in parts if j & bit]
        later = sum(bits[step + 1 :])
        for j in sorted(going, key=lambda j: not (j & later)):
            part = lax.ppermute(parts.pop(j), "term", [(i, i ^ (2 * bit)) for i in range(count)])
            if j == bit:
                arrived.append(part)
            else:
                parts[j ^ bit] = parts[j ^ bit] + part
    return arrived


def body(
    psi, precond, left_environment_block, right_env, term_operators, term_charge, sector_sizes,
    sector_energy,
):
    sectors, size, phys, _ = psi.shape
    terms = term_charge.shape[0]
    count, planes = lax.axis_size("term"), lax.axis_size("sector")
    chips = count // 2
    rows = size // count
    half = size // 2
    lanes = phys * half
    numel = sectors * planes * size * phys * size
    me = lax.axis_index("term")
    chip, core = me // 2, me % 2
    info = jnp.concatenate([jnp.stack([chip, core]).astype(jnp.int32), sector_sizes, term_charge])
    ints_a = info
    floats_a = jnp.concatenate([term_operators.reshape(-1), sector_energy])

    positions = jnp.arange(size, dtype=jnp.int32)

    any_spec = pl.BlockSpec(memory_space=pl.ANY)
    smem = pl.BlockSpec(memory_space=pltpu.SMEM)
    vmem = pl.BlockSpec(memory_space=pltpu.VMEM)
    params = pltpu.CompilerParams(vmem_limit_bytes=VMEM_BYTES)

    edge = jax.ShapeDtypeStruct((phys * half, size), F32)
    up, down = pl.pallas_call(
        send_kernel,
        out_shape=[edge] * 2,
        in_specs=[smem, any_spec],
        out_specs=[vmem] * 2,
        scratch_shapes=[pltpu.SemaphoreType.DMA((2, phys))],
        compiler_params=pltpu.CompilerParams(vmem_limit_bytes=SEND_BYTES),
        name="send",
    )(sector_sizes, psi)
    up, down, left_late, right_late = lax.optimization_barrier(
        (up, down, left_environment_block, right_env)
    )
    forward = [(i, i + 1) for i in range(planes - 1)]
    backward = [(b, a) for a, b in forward]
    low_a = lax.ppermute(up, "sector", forward)
    high_a = lax.ppermute(down, "sector", backward)

    left_a, right_a = left_environment_block, right_env
    ints_b = swap_cores(ints_a, count)
    floats_b = swap_cores(floats_a, count)
    right_b = swap_cores(right_late, count)
    left_b = swap_cores(left_late, count)

    wide = jax.ShapeDtypeStruct((sectors, size, lanes), F32)
    block = jax.ShapeDtypeStruct((sectors, 2, rows, lanes), F32)
    piece = jax.ShapeDtypeStruct((2, rows, lanes), F32)
    pair_list = pltpu.SMEM((3, 2 * terms * sectors + 1), jnp.int32)
    splits = (sectors, phys * size, 3 * size)
    near_scratch = [
        pltpu.VMEM((3 * size, half), BF16),
        pltpu.VMEM((size, 3 * size), BF16),
        pltpu.VMEM((phys * size, half), F32),
        pltpu.VMEM((3 * size, lanes), BF16),
        pair_list,
    ]

    def cost(pairs):
        return pl.CostEstimate(
            flops=pairs * 3 * 4 * size * size * lanes, bytes_accessed=12 << 20, transcendentals=0
        )

    near, state, source = pl.pallas_call(
        functools.partial(near_kernel, True, phys),
        out_shape=[wide, block, jax.ShapeDtypeStruct(splits, BF16)],
        in_specs=[smem] * 3 + [any_spec] + [vmem] * 2,
        out_specs=[vmem] * 3,
        scratch_shapes=[
            *near_scratch,
            pltpu.VMEM((sectors, phys * size, size), F32),
            pltpu.SemaphoreType.DMA((sectors, phys)),
        ],
        compiler_params=params,
        cost_estimate=cost(terms * sectors),
        name="near_own",
    )(info, ints_a, floats_a, psi, left_a, right_a)
    near = pl.pallas_call(
        functools.partial(near_kernel, False, phys),
        out_shape=wide,
        in_specs=[smem] * 3 + [vmem] * 4,
        out_specs=vmem,
        scratch_shapes=near_scratch,
        compiler_params=params,
        cost_estimate=cost(terms * sectors),
        name="near_partner",
    )(info, ints_b, floats_b, source, left_b, right_b, near)

    low_a, high_a, near = lax.optimization_barrier((low_a, high_a, near))
    low_b = swap_cores(low_a, count)
    high_b = swap_cores(high_a, count)

    def far(last, low, high, base):
        return pl.pallas_call(
            functools.partial(far_kernel, last, chips),
            out_shape=[piece] * (chips * sectors) if last else wide,
            in_specs=[smem] * 5 + [vmem] * 7,
            out_specs=[vmem] * (chips * sectors) if last else vmem,
            scratch_shapes=[
                pltpu.VMEM((2, phys * half, 3 * size), BF16),
                pltpu.VMEM((3 * size, half), BF16),
                pltpu.VMEM((phys * half, half), F32),
                pltpu.VMEM((size, 3 * half), BF16),
                pltpu.VMEM((3 * half, lanes), BF16),
                pair_list,
            ]
            + [pltpu.VMEM((sectors, size, lanes), F32)] * last,
            compiler_params=params,
            cost_estimate=cost(terms // 2),
            name="far_last" if last else "far_first",
        )(
            info, ints_a, ints_b, floats_a, floats_b, low, high, right_a, right_b, left_a, left_b,
            base,
        )

    parts = far(True, low_b, high_b, far(False, low_a, high_a, near))

    *parts, precond, sector_sizes = lax.optimization_barrier((*parts, precond, sector_sizes))

    first = chip * 2 * rows
    inside = positions[None, :] < sector_sizes[:, None]
    scale = lax.dynamic_slice(
        precond, (0, first, 0, core * half), (sectors, 2 * rows, phys, half)
    ).astype(F32)
    a = lax.dynamic_slice(inside, (0, first), (sectors, 2 * rows))
    b = lax.dynamic_slice(inside, (0, core * half), (sectors, half))
    scale = jnp.where(a[:, :, None, None] & b[:, None, None, :], 1.0 / scale, 0)
    scale = scale.reshape(sectors, 2, rows, lanes)
    scale = jnp.where(core == 0, scale, scale[:, ::-1])

    if chips > 1:
        direct = [(chips // 2 if t % 2 else 1) * sectors + t for t in range(sectors)]
        *late, scale = lax.optimization_barrier((*(parts[i] for i in direct), scale))
        for i, part in zip(direct, late):
            parts[i] = part
    parts = [sum_chips(parts[t::sectors], count, t % 2 == 1) for t in range(sectors)]

    devices = count * planes
    pair = jax.ShapeDtypeStruct((2, sectors, rows, lanes), F32)
    mine, other, sums = pl.pallas_call(
        functools.partial(update_kernel, phys, terms),
        out_shape=[pair, pair, jax.ShapeDtypeStruct((devices, 128), F32)],
        in_specs=[smem] + [vmem] * (sum(map(len, parts)) + 2),
        out_specs=[vmem] * 3,
        compiler_params=params,
        name="update",
    )(floats_a, *sum(parts, []), state, scale)
    other = swap_cores(other, count)
    sums = lax.all_to_all(sums, ("sector", "term"), 0, 0, tiled=True)
    return tuple(
        pl.pallas_call(
            functools.partial(finish_kernel, numel),
            out_shape=[
                jax.ShapeDtypeStruct((sectors, rows, phys, size), F32),
                jax.ShapeDtypeStruct((1,), F32),
            ],
            in_specs=[smem] + [vmem] * 3,
            out_specs=[any_spec, smem],
            scratch_shapes=[
                pltpu.VMEM((sectors, phys, rows, size), F32),
                pltpu.SemaphoreType.DMA((sectors, phys)),
            ],
            compiler_params=params,
            name="finish",
        )(info, sums, mine, other)
    )


def solution(mesh):
    in_specs = (
        P("sector", None, None, None),
        P("sector", None, None, None),
        P("term", "sector", None, None),
        P("term", "sector", None, None),
        P("term", None, None),
        P("term"),
        P("sector"),
        P("sector"),
    )
    out_specs = (P("sector", "term", None, None), P())
    return jax.shard_map(body, mesh=mesh, in_specs=in_specs, out_specs=out_specs, check_vma=False)
```
